128 devices in a mesh: row: 8 (over z, y_hi), col: 16 (over y_lo, x, core).
Axes of the slice: x: 4, y: 4 (y_hi: 2, y_lo: 2; y = y_hi * 2 + y_lo), z: 4, core: 2. Of those that a mesh axis runs over, the one named last changes fastest.
Arguments:
- tile_u: bfloat16 [8, 16, 2688, 256], P('row', 'col'), may hold values from -6 to 6
- tile_v: bfloat16 [8, 16, 2688, 256], P('row', 'col'), may hold values from -0.125 to 0.125
- row_u: bfloat16 [8, 2688, 256], P('row', 'col'), may hold values from -6 to 6
- row_v: bfloat16 [8, 2688, 256], P('row', 'col'), may hold values from -0.125 to 0.125
- col_u: bfloat16 [16, 2688, 64], P('col', 'row'), may hold values from -0.125 to 0.125
- col_v: bfloat16 [16, 2688, 64], P('col', 'row'), may hold values from -0.125 to 0.125
- tile_rank: int32 [8, 16], P('row', 'col'), may hold values from 32 to 256, as said below
- row_rank: int32 [8], P('row'), may hold values from 128 to 256, as said below
- col_rank: int32 [16], P('col'), may hold values from 32 to 64, as said below
- target_rank: int32 [8, 16], P('row', 'col'), may hold values from 32 to 256, as said below
- sketch: float32 [320, 256], replicated, may hold values from -6 to 6
Outputs:
- new_u: float32 [8, 16, 2688, 256], P('row', 'col')
- new_v: float32 [8, 16, 2688, 256], P('row', 'col')
The draws below stay inside these ranges and needn't reach their ends.
Inputs may be any that keep to these rules, and one draw needn't show every extreme that they name: tile_rank(i,j) is 256 for at least one tile. target_rank(i,j) is at most tile_rank(i,j), and 256 for at least one tile. Every row_rank(i) is at least every col_rank(j). Every col_rank(j) is at most every row_rank(i).
All inputs are finite; a program needn't handle non-finite values.
Results may differ from the reference program's by a relative error of at most 0.00085.
Values may be sent and summed in bfloat16 or wider, within the bound.
No kernel may reach another device: no remote copies, remote signals or barrier semaphores. Data moves between devices by JAX's collectives and lax.ppermute only.
A program may use at most 128 MiB of HBM per device.

```python
import math
import jax
import jax.numpy as jnp
from jax import lax

NB = 2688
RMAX = 256
PRANK = 64
ROW_TILES = 8
COL_TILES = 16


def rank_table(key):
    ranks = jax.random.randint(jax.random.fold_in(key, 21), (ROW_TILES, COL_TILES), RMAX // 8, RMAX + 1)
    first_spot = jax.random.randint(jax.random.fold_in(key, 22), (), 0, ROW_TILES)
    second_spot = jax.random.randint(jax.random.fold_in(key, 23), (), 0, COL_TILES)
    spot = (jnp.arange(ROW_TILES)[:, None] == first_spot) & (jnp.arange(COL_TILES)[None, :] == second_spot)
    return (jnp.where(spot, RMAX, ranks).astype(jnp.int32), spot)


def ends_fixed(key, count, lowest, highest):
    values = jax.random.randint(jax.random.fold_in(key, 41), (count,), lowest, highest + 1)
    place = jax.random.randint(jax.random.fold_in(key, 42), (), 0, count)
    index = jnp.arange(count)
    values = jnp.where(index == place, highest, values)
    values = jnp.where(index == (place + 1) % count, lowest, values)
    return values.astype(jnp.int32)


def draw_tile_rank(key, part):
    ranks, spot = rank_table(key)
    return ranks


def draw_target_rank(key, part):
    ranks, spot = rank_table(key)
    key = jax.random.fold_in(key, 7)
    picked = jax.random.randint(key, (ROW_TILES, COL_TILES), RMAX // 8, ranks + 1)
    return jnp.where(spot, RMAX, picked).astype(jnp.int32)


def draw_row_rank(key, part):
    key = jax.random.fold_in(key, 11)
    return ends_fixed(key, ROW_TILES, RMAX // 2, RMAX)


def draw_col_rank(key, part):
    key = jax.random.fold_in(key, 13)
    return ends_fixed(key, COL_TILES, RMAX // 8, PRANK)


def level_of(own_key, extent, pieces, smallest, top_value):
    def one(dim, shards_of):
        draws = jax.random.uniform(jax.random.fold_in(jax.random.fold_in(own_key, 6), dim), (shards_of,), jnp.float32, smallest / len(pieces), top_value / len(pieces))
        return jnp.repeat(jnp.exp(draws), extent[dim] // shards_of).reshape((-1,) + (1,) * (len(extent) - dim - 1))

    factor_of = one(*pieces[0])
    for cut in pieces[1:]:
        factor_of = factor_of * one(*cut)
    return factor_of


def centred(rng, shape, scale, bound, split=(), kind=jnp.bfloat16):
    result = jax.random.normal(rng, shape, jnp.float32) * scale
    if len(split) > 0:
        result = level_of(rng, shape, split, -0.22, 0.18) * result
    return jnp.clip(result, min=-bound, max=bound).astype(kind)


def setup_inputs(seed: int = 0) -> dict:
    splits = jax.random.split(jax.random.key(seed), 12)
    return {
        "tile_u": centred(splits[0], (ROW_TILES, COL_TILES, NB, RMAX), 1.0, 6.0, ((0, 8), (1, 16))),
        "tile_v": centred(splits[1], (ROW_TILES, COL_TILES, NB, RMAX), NB ** -0.5, 0.125, ((0, 8), (1, 16))),
        "row_u": centred(splits[2], (ROW_TILES, NB, RMAX), 1.0, 6.0, ((0, 8), (1, 16))),
        "row_v": centred(splits[3], (ROW_TILES, NB, RMAX), NB ** -0.5, 0.125, ((0, 8), (1, 16))),
        "col_u": centred(splits[4], (COL_TILES, NB, PRANK), NB ** -0.5, 0.125, ((0, 16), (1, 8))),
        "col_v": centred(splits[5], (COL_TILES, NB, PRANK), NB ** -0.5, 0.125, ((0, 16), (1, 8))),
        "tile_rank": draw_tile_rank(jax.random.fold_in(splits[11], 71), 0),
        "row_rank": draw_row_rank(jax.random.fold_in(splits[11], 71), 0),
        "col_rank": draw_col_rank(jax.random.fold_in(splits[11], 71), 0),
        "target_rank": draw_target_rank(jax.random.fold_in(splits[11], 71), 0),
        "sketch": centred(splits[10], (RMAX + PRANK, RMAX), 1.0, 6.0, (), jnp.float32),
    }


def high_dot(left_side, right_side):
    return jnp.dot(left_side.astype(jnp.float32), right_side.astype(jnp.float32), precision=lax.Precision.HIGHEST, preferred_element_type=jnp.float32)

def orthonormal(block, gram, live):
    lower = jnp.linalg.cholesky(gram + jnp.diag(1.0 - live))
    basis = lax.linalg.triangular_solve(lower, block, left_side=False, lower=True, transpose_a=True)
    return (basis, lower)

def recompress(left, right, gram_u, gram_v, live, keep_s, sketch, length):
    basis_u, lower_u = orthonormal(left, gram_u, live)
    basis_v, lower_v = orthonormal(right, gram_v, live)
    core = high_dot(lower_u.T, lower_v) * live[:, None] * live[None, :]
    sample = high_dot(core, sketch * keep_s[None, :])
    first, unused_a = orthonormal(sample, high_dot(sample.T, sample), keep_s)
    second, unused_b = orthonormal(first, high_dot(first.T, first), keep_s)
    fresh_u = high_dot(basis_u, second) * math.sqrt(length)
    fresh_v = high_dot(basis_v, high_dot(core.T, second))
    return (fresh_u, fresh_v)

def reference(tile_u, tile_v, row_u, row_v, col_u, col_v, tile_rank, row_rank, col_rank, target_rank, sketch):
    columns = jnp.arange(RMAX, dtype=jnp.int32)
    panel_columns = jnp.arange(PRANK, dtype=jnp.int32)

    def one_tile(index):
        first_index = (index // COL_TILES).astype(jnp.int32)
        second_index = (index % COL_TILES).astype(jnp.int32)
        keep_t = (columns < tile_rank[first_index, second_index]).astype(jnp.float32)
        keep_i = (columns < row_rank[first_index]).astype(jnp.float32)
        keep_j = (panel_columns < col_rank[second_index]).astype(jnp.float32)
        keep_s = (columns < target_rank[first_index, second_index]).astype(jnp.float32)
        cross = lax.dot_general(row_v[first_index].astype(jnp.float32), col_v[second_index].astype(jnp.float32), (((0,), (0,)), ((), ())), preferred_element_type=jnp.float32)
        cross = (cross * keep_i[:, None] * keep_j[None, :]).astype(jnp.bfloat16)
        update = jnp.dot(row_u[first_index].astype(jnp.float32), cross.astype(jnp.float32), preferred_element_type=jnp.float32)
        own_u = tile_u[first_index, second_index].astype(jnp.float32) * keep_t[None, :]
        own_v = tile_v[first_index, second_index].astype(jnp.float32) * keep_t[None, :]
        left = jnp.concatenate([own_u, update], axis=1)
        right = jnp.concatenate([own_v, -col_u[second_index].astype(jnp.float32) * keep_j[None, :]], axis=1)
        live = jnp.concatenate([keep_t, keep_j])
        return recompress(left, right, high_dot(left.T, left), high_dot(right.T, right), live, keep_s, sketch, NB)
    fresh_u, fresh_v = lax.map(one_tile, jnp.arange(ROW_TILES * COL_TILES, dtype=jnp.int32))
    return (fresh_u.reshape(ROW_TILES, COL_TILES, NB, RMAX), fresh_v.reshape(ROW_TILES, COL_TILES, NB, RMAX))
```

```python
import math

import jax
import jax.numpy as jnp
from jax import lax
from jax.experimental import pallas as pl
from jax.experimental.pallas import tpu as pltpu
from jax.sharding import PartitionSpec as P

F32 = jnp.float32
BF16 = jnp.bfloat16
HIGH = lax.Precision.HIGHEST


def nn(a, b, precision=HIGH):
    return lax.dot_general(a, b, (((1,), (0,)), ((), ())), precision=precision, preferred_element_type=F32)


def nt(a, b, precision=HIGH):
    return lax.dot_general(a, b, (((1,), (1,)), ((), ())), precision=precision, preferred_element_type=F32)


def tn(a, b, precision=None):
    return lax.dot_general(a, b, (((0,), (0,)), ((), ())), precision=precision, preferred_element_type=F32)


def lane_splat(x, lane):
    return jnp.broadcast_to(x[:, lane : lane + 1], x.shape)


def row_splat(x, row):
    return jnp.broadcast_to(x[row : row + 1, :], x.shape)


def total(terms):
    while len(terms) > 1:
        terms = [terms[k] + terms[k + 1] if k + 1 < len(terms) else terms[k] for k in range(0, len(terms), 2)]
    return terms[0]


def leaf(block):
    rows = [block[8 * r : 8 * r + 8, :] for r in range(8)]
    sub = lax.broadcasted_iota(jnp.int32, (8, 128), 0)
    for b in range(8):
        cols = {r: [lane_splat(rows[r], 64 + 8 * b + m) for m in range(8)] for r in range(b, 8)}
        a = {(s, m): row_splat(cols[b][m], s) for m in range(8) for s in range(m, 8)}
        own = [row_splat(rows[b], m) for m in range(8)]
        low = {}
        inv = {}
        for k in range(8):
            scale = lax.rsqrt(a[k, k])
            inv[k, k] = scale
            for i in range(k + 1, 8):
                low[i, k] = a[i, k] * scale
            for j in range(k + 1, 8):
                for i in range(j, 8):
                    a[i, j] = a[i, j] - low[i, k] * low[j, k]
        for m in range(8):
            for i in range(m + 1, 8):
                inv[i, m] = -inv[i, i] * total([low[i, q] * inv[q, m] for q in range(m, i)])
        up = [total([inv[n, m] * own[m] for m in range(n + 1)]) for n in range(8)]
        if b < 7:
            back = [total([inv[n, m] * up[n] for n in range(m, 8)]) for m in range(8)]
            for r in range(b + 1, 8):
                rows[r] = rows[r] - total([cols[r][m] * back[m] for m in range(8)])
        own_rows = up[0]
        for n in range(1, 8):
            own_rows = jnp.where(sub == n, up[n], own_rows)
        rows[b] = own_rows
    return jnp.concatenate(rows, axis=0)


def shifted(pair):
    lane = lax.broadcasted_iota(jnp.int32, pair.shape, 1)
    return jnp.where(lane >= 64, pltpu.roll(pair, 64, 1), 0.0)


def spread(matrix, aug_ref):
    size = matrix.shape[0]
    lane = lax.broadcasted_iota(jnp.int32, (size, 128), 1)
    row = lax.broadcasted_iota(jnp.int32, (size, 128), 0)
    for k in range(size // 64):
        half = matrix[:, 128 * (k // 2) : 128 * (k // 2) + 128]
        if k % 2 == 0:
            half = pltpu.roll(half, 64, 1)
        eye = (row == lane + 64 * k).astype(F32)
        aug_ref[:, 128 * k : 128 * k + 128] = jnp.where(lane >= 64, half, eye)


def gather_inverse(aug_ref):
    lane = lax.broadcasted_iota(jnp.int32, (aug_ref.shape[0], 128), 1)
    parts = []
    for t in range(aug_ref.shape[1] // 256):
        even = aug_ref[:, 256 * t : 256 * t + 128]
        odd = aug_ref[:, 256 * t + 128 : 256 * t + 256]
        parts.append(jnp.where(lane < 64, even, pltpu.roll(odd, 64, 1)))
    return jnp.concatenate(parts, axis=1)


def factor(aug_ref, low_refs=None):
    size = aug_ref.shape[0]
    for k in range(size // 64):
        here = slice(64 * k, 64 * k + 64)
        tile = slice(128 * k, 128 * k + 128)
        pair = leaf(aug_ref[here, tile])
        wide = shifted(pair)
        first = 64 * k if low_refs is not None else 64 * k + 64
        if first < size:
            left = nt(aug_ref[first:, tile], wide)
        ahead = nn(pair[:, :64], aug_ref[here, :])
        aug_ref[here, :] = ahead
        if low_refs is not None:
            low_refs[k][64 * k :, :] = left
            left = left[64:]
        if 64 * k + 64 < size:
            aug_ref[64 * k + 64 :, :] = aug_ref[64 * k + 64 :, :] - nn(left, ahead)


def masked_gram(gram, rank):
    size = gram.shape[0]
    row = lax.broadcasted_iota(jnp.int32, gram.shape, 0)
    col = lax.broadcasted_iota(jnp.int32, gram.shape, 1)
    both = (row < rank) & (col < rank)
    dead = (row == col) & (row >= rank)
    return jnp.where(both, gram, 0.0), dead.astype(F32)


def own_kernel(ranks, tile_u, tile_v, gram_u, low, low_inv, aug_ref, l0, l1, l2, l3):
    rank = ranks[0]
    plain, dead = masked_gram(tn(tile_v[...], tile_v[...]), rank)
    spread(plain + dead, aug_ref)
    plain_u, unused = masked_gram(tn(tile_u[...], tile_u[...]), rank)
    gram_u[...] = plain_u
    lows = (l0, l1, l2, l3)
    factor(aug_ref, lows)
    low_inv[...] = gather_inverse(aug_ref)
    row = lax.broadcasted_iota(jnp.int32, (256, 256), 0)
    col = lax.broadcasted_iota(jnp.int32, (256, 256), 1)
    joined = jnp.concatenate([l0[...], l1[...], l2[...], l3[...]], axis=1)
    low[...] = jnp.where(row >= col, joined, 0.0)


def own_call(ranks, tile_u, tile_v):
    square = jax.ShapeDtypeStruct((256, 256), F32)
    vmem = pl.BlockSpec(memory_space=pltpu.VMEM)
    return pl.pallas_call(
        own_kernel,
        out_shape=(square,) * 3,
        in_specs=[pl.BlockSpec(memory_space=pltpu.SMEM), vmem, vmem],
        out_specs=(vmem,) * 3,
        scratch_shapes=[pltpu.VMEM((256, 512), F32)] + [pltpu.VMEM((256, 64), F32)] * 4,
        compiler_params=pltpu.CompilerParams(vmem_limit_bytes=40 * 1024 * 1024),
        cost_estimate=pl.CostEstimate(flops=20 * 10**9, bytes_accessed=4 * 10**6, transcendentals=0),
        name="own_factor",
    )(ranks, tile_u, tile_v)


CHUNK = 336
SHIFTS = (0, 1, 3, 2)
TOLERANCE = 3e-4


def main_kernel(ranks, gram_tt, low, low_inv, sketch_t, tile_u_hbm, tile_v_hbm, mine_hbm, other_hbm, side0, side1, side2, side3,
                out_u_hbm, out_v_hbm,
                tile_u, tile_v, panel, col_uv, up, wide_u, out_u, out_v, aug_ref, w_t, w_p, g_t, g_p,
                in_sem, out_sem):
    rows = tile_u.shape[0]
    block = side0.shape[1]

    def place(first, second):
        return pl.ds(pl.multiple_of((first * 4 + second) * block, block), block)

    mine, high, z, x = ranks[4], ranks[5], ranks[6], ranks[7]
    y_half = ranks[8]
    side_loads = []
    for hop, side in enumerate((side0, side1, side2, side3)):
        for k in range(2):
            start = (lax.rem(z - SHIFTS[hop] + 4, 4) * 2 + lax.rem(y_half + k, 2)) * block
            spot = pl.ds(pl.multiple_of(start, block), block)
            side_loads.append(pltpu.make_async_copy(side.at[k], col_uv.at[spot, :], in_sem.at[2 * hop + k]))
    row_loads = []
    for which, array in enumerate((mine_hbm, other_hbm)):
        slot = lax.rem(mine + which, 2)
        for hop in range(4):
            for k in range(2):
                spot = place(lax.rem(high + k, 2), lax.rem(x - SHIFTS[hop] + 4, 4))
                sem = in_sem.at[8 + 8 * which + 2 * hop + k]
                row_loads.append(pltpu.make_async_copy(array.at[hop, k], panel.at[slot, spot, :], sem))
    load_v = pltpu.make_async_copy(tile_v_hbm, tile_v, in_sem.at[24])
    load_u = pltpu.make_async_copy(tile_u_hbm, tile_u, in_sem.at[25])
    for load in side_loads + [load_v] + row_loads + [load_u]:
        load.start()
    t_rank, i_rank, j_rank, s_rank = ranks[0], ranks[1], ranks[2], ranks[3]
    iota = lambda shape, dim: lax.broadcasted_iota(jnp.int32, shape, dim)
    for load in side_loads + [load_v]:
        load.wait()
    both = col_uv[...]
    mask_pt = (iota((64, 256), 0) < j_rank) & (iota((64, 256), 1) < t_rank)
    side = jnp.where(mask_pt, -tn(both, tile_v[...])[:64], 0.0)
    corner, dead = masked_gram(tn(both, both)[:64, :64], j_rank)
    low_pt = nt(side, low_inv[...])
    schur = corner + dead - nt(low_pt, low_pt)
    eye = (iota((64, 64), 0) == iota((64, 64), 1)).astype(F32)
    start = jnp.concatenate([eye, schur], axis=1)
    pair = leaf(start)
    low_pp = nt(start, shifted(pair))
    low_pp = jnp.where(iota((64, 64), 0) >= iota((64, 64), 1), low_pp, 0.0)
    keep_rows = iota((256, 320), 0) < s_rank
    st = jnp.where(keep_rows, sketch_t[...], 0.0)
    st_t, st_p = st[:, :256], st[:, 256:]
    keep_tt = iota((256, 256), 1) < t_rank
    keep_tp = iota((256, 64), 1) < j_rank
    y_t = jnp.where(keep_tt, nt(st_t, low[...]), 0.0)
    y_p = jnp.where(keep_tp, nt(st_t, low_pt) + nt(st_p, low_pp), 0.0)
    for load in row_loads:
        load.wait()
    mask_ij = (iota((64, 256), 0) < j_rank) & (iota((64, 256), 1) < i_rank)
    cross_t = jnp.where(mask_ij, tn(col_uv[...], panel[1])[64:], 0.0).astype(BF16)

    def expand(step, carry):
        here = pl.ds(pl.multiple_of(step * CHUNK, CHUNK), CHUNK)
        update = nt(panel[0, here, :], cross_t, None)
        top = update.astype(BF16)
        rest = (update - top.astype(F32)).astype(BF16)
        up[here, :] = jnp.concatenate([top, rest], axis=1)
        side_u = col_uv[here, :][:, :64]
        wide_u[here, :] = jnp.concatenate([side_u, side_u], axis=1)
        return carry

    lax.fori_loop(0, rows // CHUNK, expand, 0)
    load_u.wait()
    both_t = tn(up[...], tile_u[...])
    gram_pt = jnp.where(mask_pt, both_t[:64] + both_t[64:], 0.0)
    four = tn(up[...], up[...])
    four = four[:64] + four[64:]
    gram_pp = (four + pltpu.roll(four, 64, 1))[:, :64]
    x_t = nn(y_t, gram_tt[...]) + nn(y_p, gram_pt)
    x_p = nt(y_t, gram_pt) + nn(y_p, gram_pp)
    middle = nt(x_t, y_t) + nt(x_p, y_p)
    same = iota((256, 256), 0) == iota((256, 256), 1)
    off = (iota((256, 256), 0) >= s_rank) & same
    spread(middle + off.astype(F32), aug_ref)
    factor(aug_ref)
    inverse = gather_inverse(aug_ref)
    w_t[...] = nn(inverse, y_t)
    w_p[...] = nn(inverse, y_p)
    g_t[...] = nn(inverse, x_t)
    g_p[...] = nn(inverse, x_p)
    live = (iota((256, 256), 0) < s_rank) & same
    lower = jnp.where(iota((256, 256), 0) > iota((256, 256), 1), 1.0, 0.0) + jnp.where(same, 0.5, 0.0)

    def refine(state):
        count, unused = state
        error = nt(w_t[...], g_t[...]) + nt(w_p[...], g_p[...]) - live.astype(F32)
        size = jnp.max(jnp.sum(jnp.abs(error), axis=1, keepdims=True))
        error = error * lower
        for ref in (w_t, w_p, g_t, g_p):
            ref[...] = ref[...] - nn(error, ref[...])
        return count + 1, size

    lax.while_loop(lambda s: (s[0] < 12) & (s[1] > TOLERANCE), refine, (jnp.int32(0), jnp.float32(1.0)))
    scale = math.sqrt(rows)

    def halves(x):
        top = x.astype(BF16)
        return top, (x - top.astype(F32)).astype(BF16)

    u_hi, u_lo = halves(w_t[...] * scale)
    p_hi, p_lo = halves(w_p[...] * scale)
    p_hi2 = jnp.concatenate([p_hi, p_hi], axis=1)
    p_lo2 = jnp.concatenate([p_lo, p_lo], axis=1)
    v_hi, v_lo = halves(g_t[...])
    q2 = jnp.concatenate(halves(-g_p[...]), axis=1)

    def send(step, carry):
        here = pl.ds(pl.multiple_of(step * CHUNK, CHUNK), CHUNK)
        tile = tile_u[here, :]
        extra = up[here, :]
        out_u[here, :] = nt(tile, u_hi, None) + nt(tile, u_lo, None) + nt(extra, p_hi2, None) + nt(extra, p_lo2, None)
        pltpu.make_async_copy(out_u.at[here, :], out_u_hbm.at[here, :], out_sem.at[0, step]).start()
        tile = tile_v[here, :]
        out_v[here, :] = nt(tile, v_hi, None) + nt(tile, v_lo, None) + nt(wide_u[here, :], q2, None)
        pltpu.make_async_copy(out_v.at[here, :], out_v_hbm.at[here, :], out_sem.at[1, step]).start()
        return carry

    lax.fori_loop(0, rows // CHUNK, send, 0)
    for step in range(rows // CHUNK):
        here = pl.ds(step * CHUNK, CHUNK)
        pltpu.make_async_copy(out_u.at[here, :], out_u_hbm.at[here, :], out_sem.at[0, step]).wait()
        pltpu.make_async_copy(out_v.at[here, :], out_v_hbm.at[here, :], out_sem.at[1, step]).wait()


def main_call(ranks, gram_tt, low, low_inv, sketch_t, tile_u, tile_v, mine, other, sides):
    rows = tile_u.shape[0]
    vmem = pl.BlockSpec(memory_space=pltpu.VMEM)
    hbm = pl.BlockSpec(memory_space=pl.ANY)
    out = jax.ShapeDtypeStruct((rows, 256), F32)
    wide = pltpu.VMEM((rows, 256), BF16)
    thin = pltpu.VMEM((rows, 128), BF16)
    return pl.pallas_call(
        main_kernel,
        out_shape=(out, out),
        in_specs=[pl.BlockSpec(memory_space=pltpu.SMEM)] + [vmem] * 4 + [hbm] * 8,
        out_specs=(hbm, hbm),
        scratch_shapes=[wide, wide, pltpu.VMEM((2, rows, 256), BF16), thin, thin, thin,
                        pltpu.VMEM((rows, 256), F32), pltpu.VMEM((rows, 256), F32), pltpu.VMEM((256, 512), F32),
                        pltpu.VMEM((256, 256), F32), pltpu.VMEM((256, 64), F32), pltpu.VMEM((256, 256), F32), pltpu.VMEM((256, 64), F32),
                        pltpu.SemaphoreType.DMA((26,)), pltpu.SemaphoreType.DMA((2, rows // CHUNK))],
        compiler_params=pltpu.CompilerParams(vmem_limit_bytes=48 * 1024 * 1024),
        cost_estimate=pl.CostEstimate(flops=20 * 10**9, bytes_accessed=15 * 10**6, transcendentals=0),
        name="recompress",
    )(ranks, gram_tt, low, low_inv, sketch_t, tile_u, tile_v, mine, other, *sides)


def send(x, axis, count, step):
    return lax.ppermute(x, axis, [(i, step(i)) for i in range(count)])


def body(tile_u, tile_v, row_u, row_v, col_u, col_v, tile_rank, row_rank, col_rank, target_rank, sketch):
    spot_i, spot_j = lax.axis_index("row"), lax.axis_index("col")
    core, x, y_low = spot_j % 2, spot_j // 2 % 4, spot_j // 8
    z, y_half = spot_i // 2, spot_i % 2
    first = core == 0
    side = jnp.concatenate([col_u[0], col_v[0]], axis=1)
    side_other = send(side, "row", 8, lambda i: i ^ 1)
    give = jnp.where(first, row_v[0], row_u[0])
    keep = jnp.where(first, row_u[0], row_v[0])
    got = send(give, "col", 16, lambda i: i ^ 1)
    chip = jnp.concatenate([jnp.where(first, keep, got), jnp.where(first, got, keep)], axis=0)
    chip_other = send(chip, "col", 16, lambda i: i ^ 8)
    ranks = jnp.stack([tile_rank[0, 0], row_rank[0], col_rank[0], target_rank[0, 0], core, y_low, z, x, y_half]).astype(jnp.int32)
    gram_tt, low, low_inv = own_call(ranks, tile_u[0, 0], tile_v[0, 0])
    side_other, chip_other = lax.optimization_barrier((side_other, chip_other))
    sides = [jnp.stack([side, side_other])]
    chips = [jnp.stack([chip, chip_other])]
    for shift in SHIFTS[1:]:
        sides.append(send(sides[0], "row", 8, lambda i: (i + 2 * shift) % 8))
        chips.append(send(chips[0], "col", 16, lambda i: i // 8 * 8 + (i + 2 * shift) % 8))
    mine = jnp.stack(chips)
    other = send(mine, "col", 16, lambda i: i ^ 1)
    new_u, new_v = main_call(ranks, gram_tt, low, low_inv, sketch.T, tile_u[0, 0], tile_v[0, 0], mine, other, sides)
    return (new_u[None, None], new_v[None, None])


def solution(mesh):
    placed = (
        P("row", "col", None, None),
        P("row", "col", None, None),
        P("row", "col", None),
        P("row", "col", None),
        P("col", "row", None),
        P("col", "row", None),
        P("row", "col"),
        P("row"),
        P("col"),
        P("row", "col"),
        P(),
    )
    return jax.shard_map(
        body,
        mesh=mesh,
        in_specs=placed,
        out_specs=(P("row", "col", None, None), P("row", "col", None, None)),
        check_vma=False,
    )
```

```python
import math

import jax
import jax.numpy as jnp
from jax import lax
from jax.experimental import pallas as pl
from jax.experimental.pallas import tpu as pltpu
from jax.sharding import PartitionSpec as P

F32 = jnp.float32
BF16 = jnp.bfloat16
HIGH = lax.Precision.HIGHEST
CHUNK = 896
TOLERANCE = 3e-4
SHIFTS = (0, 1, 3, 2)
VMEM_LIMIT = 60 * 1024 * 1024


def nn(a, b, precision=HIGH):
    return lax.dot_general(a, b, (((1,), (0,)), ((), ())), precision=precision, preferred_element_type=F32)


def nt(a, b, precision=HIGH):
    return lax.dot_general(a, b, (((1,), (1,)), ((), ())), precision=precision, preferred_element_type=F32)


def tn(a, b, precision=None):
    return lax.dot_general(a, b, (((0,), (0,)), ((), ())), precision=precision, preferred_element_type=F32)


def lane_splat(x, lane):
    return jnp.broadcast_to(x[:, lane : lane + 1], x.shape)


def row_splat(x, row):
    return jnp.broadcast_to(x[row : row + 1, :], x.shape)


def total(terms):
    while len(terms) > 1:
        terms = [terms[k] + terms[k + 1] if k + 1 < len(terms) else terms[k] for k in range(0, len(terms), 2)]
    return terms[0]


def leaf(block):
    count = 8
    rows = [block[8 * r : 8 * r + 8, :] for r in range(count)]
    sub = lax.broadcasted_iota(jnp.int32, (8, 128), 0)
    diag = [lane_splat(rows[0], 64 + m) for m in range(8)]
    for b in range(count):
        more = b + 1 < count
        x = rows[b]
        if more:
            ahead = rows[b + 1]
            side = [lane_splat(ahead, 64 + 8 * b + m) for m in range(8)]
            following = [lane_splat(ahead, 72 + 8 * b + m) for m in range(8)]
        far = {r: [lane_splat(rows[r], 64 + 8 * b + m) for m in range(8)] for r in range(b + 2, count)}
        inverse, pivot_rows, low = [], [], []
        pivots = diag[0]
        for k in range(8):
            r = 1.0 / row_splat(diag[k], k)
            inverse.append(r)
            if k:
                pivots = jnp.where(sub == k, diag[k], pivots)
            below = jnp.where(sub > k, diag[k], 0.0)
            low.append(below)
            pivot = row_splat(x, k) * r
            pivot_rows.append(pivot)
            for m in range(k + 1, 8):
                entry = row_splat(diag[m], k)
                diag[m] = diag[m] - (below * entry) * r
                if more:
                    side[m] = side[m] - side[k] * (entry * r)
            x = x - below * pivot
            if more:
                ahead = ahead - side[k] * pivot
        if more:
            scaled = [side[k] * inverse[k] for k in range(8)]
            diag = [
                following[m] - total([scaled[k] * row_splat(side[k], m) for k in range(8)]) for m in range(8)
            ]
            rows[b + 1] = ahead
        if far:
            back = [None] * 8
            for k in range(7, -1, -1):
                column = low[k] * inverse[k]
                back[k] = pivot_rows[k]
                for i in range(k + 1, 8):
                    back[k] = back[k] - row_splat(column, i) * back[i]
            for r in far:
                rows[r] = rows[r] - total([far[r][m] * back[m] for m in range(8)])
        rows[b] = x * lax.rsqrt(pivots)
    return jnp.concatenate(rows, axis=0)


def shifted(pair):
    lane = lax.broadcasted_iota(jnp.int32, pair.shape, 1)
    return jnp.where(lane >= 64, pltpu.roll(pair, 64, 1), 0.0)


def spread(matrix, aug_ref):
    size = matrix.shape[0]
    lane = lax.broadcasted_iota(jnp.int32, (size, 128), 1)
    row = lax.broadcasted_iota(jnp.int32, (size, 128), 0)
    for k in range(size // 64):
        half = matrix[:, 128 * (k // 2) : 128 * (k // 2) + 128]
        if k % 2 == 0:
            half = pltpu.roll(half, 64, 1)
        eye = (row == lane + 64 * k).astype(F32)
        aug_ref[:, 128 * k : 128 * k + 128] = jnp.where(lane >= 64, half, eye)


def gather_inverse(aug_ref):
    lane = lax.broadcasted_iota(jnp.int32, (aug_ref.shape[0], 128), 1)
    parts = []
    for t in range(aug_ref.shape[1] // 256):
        even = aug_ref[:, 256 * t : 256 * t + 128]
        odd = aug_ref[:, 256 * t + 128 : 256 * t + 256]
        parts.append(jnp.where(lane < 64, even, pltpu.roll(odd, 64, 1)))
    return jnp.concatenate(parts, axis=1)


def factor(aug_ref, low_refs=None):
    size = aug_ref.shape[0]
    count = size // 64
    start = aug_ref[:64, :128]
    for k in range(count):
        here = slice(64 * k, 64 * k + 64)
        tile = slice(128 * k, 128 * k + 128)
        pair = leaf(start)
        wide = shifted(pair)
        inverse = pair[:, :64]
        if low_refs is not None:
            low_refs[k][here, :] = nt(start, wide)
        if k + 1 == count:
            aug_ref[here, :] = nn(inverse, aug_ref[here, :])
            break
        below = slice(64 * k + 64, 64 * k + 128)
        after = slice(128 * k + 128, 128 * k + 256)
        near = nt(aug_ref[below, tile], wide)
        start = aug_ref[below, after] - nn(near, nn(inverse, aug_ref[here, after]))
        ahead = nn(inverse, aug_ref[here, :])
        left = nt(aug_ref[64 * k + 64 :, tile], wide)
        aug_ref[here, :] = ahead
        if low_refs is not None:
            low_refs[k][64 * k + 64 :, :] = left
        aug_ref[64 * k + 64 :, :] = aug_ref[64 * k + 64 :, :] - nn(left, ahead)


def masked_gram(gram, rank):
    size = gram.shape[0]
    row = lax.broadcasted_iota(jnp.int32, gram.shape, 0)
    col = lax.broadcasted_iota(jnp.int32, gram.shape, 1)
    both = (row < rank) & (col < rank)
    dead = (row == col) & (row >= rank)
    return jnp.where(both, gram, 0.0), dead.astype(F32)


def iota(shape, dim):
    return lax.broadcasted_iota(jnp.int32, shape, dim)


def halves(x):
    top = x.astype(BF16)
    return top, (x - top.astype(F32)).astype(BF16)


def lower_only(x):
    return jnp.where(iota(x.shape, 0) >= iota(x.shape, 1), x, 0.0)


def copy_all(pairs, sem):
    copies = [pltpu.make_async_copy(source, target, sem.at[k]) for k, (source, target) in enumerate(pairs)]
    for copy in copies:
        copy.start()
    return copies


def own_kernel(
    ranks, sketch_hbm, tile_u_hbm, tile_v_hbm,
    low_inv_hbm, sketch_t_hbm, y_hbm, x_hbm,
    sketch, tile_u, tile_v, aug_ref, low0, low1, low2, low3, low_inv, sketch_t, y_ref, x_ref,
    in_sem, out_sem,
):
    loads = copy_all([(tile_v_hbm, tile_v), (tile_u_hbm, tile_u), (sketch_hbm, sketch)], in_sem)
    rank = ranks[0]
    loads[0].wait()
    gram_v, dead = masked_gram(tn(tile_v[...], tile_v[...]), rank)
    spread(gram_v + dead, aug_ref)
    loads[1].wait()
    gram_u, unused = masked_gram(tn(tile_u[...], tile_u[...]), rank)
    loads[2].wait()
    flipped = sketch[...].T
    flipped = jnp.where(iota(flipped.shape, 0) < ranks[3], flipped, 0.0)
    sketch_t[...] = flipped
    lows = (low0, low1, low2, low3)
    factor(aug_ref, lows)
    low_inv[...] = gather_inverse(aug_ref)
    for k in range(1, 4):
        lows[k][: 64 * k, :] = jnp.zeros((64 * k, 64), F32)
    low = lower_only(jnp.concatenate([ref[...] for ref in lows], axis=1))
    y = jnp.where(iota((256, 256), 1) < rank, nt(flipped[:, :256], low), 0.0)
    y_ref[...] = y
    x_ref[...] = nn(y, gram_u)
    stores = copy_all([(low_inv, low_inv_hbm), (sketch_t, sketch_t_hbm), (y_ref, y_hbm), (x_ref, x_hbm)], out_sem)
    for store in stores:
        store.wait()


def own_call(ranks, sketch, tile_u, tile_v):
    square = jax.ShapeDtypeStruct((256, 256), F32)
    wide = pltpu.VMEM(tile_u.shape, BF16)
    block = pltpu.VMEM((256, 256), F32)
    hbm = pl.BlockSpec(memory_space=pl.ANY)
    return pl.pallas_call(
        own_kernel,
        out_shape=(square, jax.ShapeDtypeStruct((256, 320), F32), square, square),
        in_specs=[pl.BlockSpec(memory_space=pltpu.SMEM)] + [hbm] * 3,
        out_specs=(hbm,) * 4,
        scratch_shapes=[pltpu.VMEM((320, 256), F32), wide, wide, pltpu.VMEM((256, 512), F32)]
        + [pltpu.VMEM((256, 64), F32)] * 4
        + [block, pltpu.VMEM((256, 320), F32), block, block, pltpu.SemaphoreType.DMA((3,)), pltpu.SemaphoreType.DMA((4,))],
        compiler_params=pltpu.CompilerParams(vmem_limit_bytes=VMEM_LIMIT),
        cost_estimate=pl.CostEstimate(flops=14 * 10**9, bytes_accessed=4 * 10**6, transcendentals=0),
        name="own_factor",
    )(ranks, sketch, tile_u, tile_v)


def side_copies(ranks, sides, target, sem, base):
    block = sides[0].shape[1]
    z, y_half = ranks[6], ranks[8]
    copies = []
    for hop, side in enumerate(sides):
        for k in range(2):
            start = (lax.rem(z - SHIFTS[hop] + 4, 4) * 2 + lax.rem(y_half + k, 2)) * block
            spot = pl.ds(pl.multiple_of(start, block), block)
            copies.append(pltpu.make_async_copy(side.at[k], target.at[spot, :], sem.at[base + 2 * hop + k]))
    return copies


def side_kernel(
    ranks, low_inv_hbm, sketch_t_hbm, tile_v_hbm, side0, side1, side2, side3,
    y_hbm,
    low_inv, sketch_t, tile_v, col_uv, y_ref, in_sem, out_sem,
):
    loads = side_copies(ranks, (side0, side1, side2, side3), col_uv, in_sem, 3)
    loads.append(pltpu.make_async_copy(tile_v_hbm, tile_v, in_sem.at[2]))
    small = [
        pltpu.make_async_copy(low_inv_hbm, low_inv, in_sem.at[0]),
        pltpu.make_async_copy(sketch_t_hbm, sketch_t, in_sem.at[1]),
    ]
    for load in loads + small:
        load.start()
    for load in loads:
        load.wait()
    t_rank, j_rank = ranks[0], ranks[2]
    both = col_uv[...]
    keep = (iota((64, 256), 0) < j_rank) & (iota((64, 256), 1) < t_rank)
    side = jnp.where(keep, -tn(both, tile_v[...])[:64], 0.0)
    corner, dead = masked_gram(tn(both, both)[:64, :64], j_rank)
    for load in small:
        load.wait()
    low_pt = nt(side, low_inv[...])
    schur = corner + dead - nt(low_pt, low_pt)
    eye = (iota((64, 64), 0) == iota((64, 64), 1)).astype(F32)
    start = jnp.concatenate([eye, schur], axis=1)
    low_pp = lower_only(nt(start, shifted(leaf(start))))
    y = nt(sketch_t[:, :256], low_pt) + nt(sketch_t[:, 256:], low_pp)
    y_ref[...] = jnp.where(iota((256, 64), 1) < j_rank, y, 0.0)
    store = pltpu.make_async_copy(y_ref, y_hbm, out_sem)
    store.start()
    store.wait()


def side_call(ranks, low_inv, sketch_t, tile_v, sides):
    hbm = pl.BlockSpec(memory_space=pl.ANY)
    rows = tile_v.shape[0]
    return pl.pallas_call(
        side_kernel,
        out_shape=jax.ShapeDtypeStruct((256, 64), F32),
        in_specs=[pl.BlockSpec(memory_space=pltpu.SMEM)] + [hbm] * 7,
        out_specs=hbm,
        scratch_shapes=[
            pltpu.VMEM((256, 256), F32), pltpu.VMEM((256, 320), F32), pltpu.VMEM((rows, 256), BF16),
            pltpu.VMEM((rows, 128), BF16), pltpu.VMEM((256, 64), F32),
            pltpu.SemaphoreType.DMA((11,)), pltpu.SemaphoreType.DMA,
        ],
        compiler_params=pltpu.CompilerParams(vmem_limit_bytes=VMEM_LIMIT),
        cost_estimate=pl.CostEstimate(flops=5 * 10**9, bytes_accessed=2 * 10**6, transcendentals=0),
        name="side_factor",
    )(ranks, low_inv, sketch_t, tile_v, *sides)


def main_kernel(
    ranks, y_t_hbm, x_t_hbm, y_p_hbm, tile_u_hbm, tile_v_hbm,
    mine0, mine1, mine2, mine3, other0, other1, other2, other3, side0, side1, side2, side3,
    out_u_hbm, out_v_hbm,
    y_t, x_t, y_p, tile_u, tile_v, panel, col_uv, up, wide_u, out_u, out_v, aug_ref, w_t, w_p, g_t, g_p,
    in_sem, out_sem,
):
    rows = tile_u.shape[0]
    t_rank, i_rank, j_rank, s_rank = ranks[0], ranks[1], ranks[2], ranks[3]
    core, y_low, x = ranks[4], ranks[5], ranks[7]
    side_loads = side_copies(ranks, (side0, side1, side2, side3), col_uv, in_sem, 0)
    row_loads = []
    block = mine0.shape[1]
    for which, arrays in enumerate(((mine0, mine1, mine2, mine3), (other0, other1, other2, other3))):
        slot = lax.rem(core + which, 2)
        for hop in range(4):
            for k in range(2):
                start = (lax.rem(y_low + k, 2) * 4 + lax.rem(x - SHIFTS[hop] + 4, 4)) * block
                spot = pl.ds(pl.multiple_of(start, block), block)
                sem = in_sem.at[8 + 8 * which + 2 * hop + k]
                row_loads.append(pltpu.make_async_copy(arrays[hop].at[k], panel.at[slot, spot, :], sem))
    load_u = pltpu.make_async_copy(tile_u_hbm, tile_u, in_sem.at[24])
    small = [
        pltpu.make_async_copy(source, target, in_sem.at[26 + k])
        for k, (source, target) in enumerate([(y_t_hbm, y_t), (x_t_hbm, x_t), (y_p_hbm, y_p)])
    ]
    load_v = pltpu.make_async_copy(tile_v_hbm, tile_v, in_sem.at[25])
    for load in side_loads + row_loads + [load_u] + small + [load_v]:
        load.start()
    for load in side_loads + row_loads:
        load.wait()
    keep = (iota((64, 256), 0) < j_rank) & (iota((64, 256), 1) < i_rank)
    cross_t = jnp.where(keep, tn(col_uv[...], panel[1])[64:], 0.0).astype(BF16)
    for step in range(rows // CHUNK):
        here = slice(step * CHUNK, step * CHUNK + CHUNK)
        top, rest = halves(nt(panel[0, here, :], cross_t, None))
        up[here, :] = jnp.concatenate([top, rest, top, rest], axis=1)
        part = col_uv[here, :][:, :64]
        wide_u[here, :] = jnp.concatenate([part, part], axis=1)
    load_u.wait()
    both = tn(up[:, :128], tile_u[...])
    keep = (iota((64, 256), 0) < j_rank) & (iota((64, 256), 1) < t_rank)
    gram_pt = jnp.where(keep, both[:64] + both[64:], 0.0)
    four = tn(up[:, :128], up[:, :128])
    four = four[:64] + four[64:]
    gram_pp = (four + pltpu.roll(four, 64, 1))[:, :64]
    for load in small:
        load.wait()
    ys, yp = y_t[...], y_p[...]
    xs = x_t[...] + nn(yp, gram_pt)
    xp = nt(ys, gram_pt) + nn(yp, gram_pp)
    same = iota((256, 256), 0) == iota((256, 256), 1)
    dead = (same & (iota((256, 256), 0) >= s_rank)).astype(F32)
    spread(nt(xs, ys) + nt(xp, yp) + dead, aug_ref)
    factor(aug_ref)
    inverse = gather_inverse(aug_ref)
    w_t[...] = nn(inverse, ys)
    w_p[...] = nn(inverse, yp)
    g_t[...] = nn(inverse, xs)
    g_p[...] = nn(inverse, xp)
    live = (same & (iota((256, 256), 0) < s_rank)).astype(F32)

    def refine(state):
        count, unused = state
        error = nt(w_t[...], g_t[...]) + nt(w_p[...], g_p[...]) - live
        size = jnp.max(jnp.sum(jnp.abs(error), axis=1, keepdims=True))
        step = lower_only(error) - jnp.where(same, 0.5 * error, 0.0)
        for ref in (w_t, w_p, g_t, g_p):
            ref[...] = ref[...] - nn(step, ref[...])
        return count + 1, size

    lax.while_loop(lambda s: (s[0] < 12) & (s[1] > TOLERANCE), refine, (jnp.int32(0), jnp.float32(1.0)))
    scale = math.sqrt(rows)
    u_hi, u_lo = halves(w_t[...] * scale)
    p_hi, p_lo = halves(w_p[...] * scale)
    p_all = jnp.concatenate([p_hi, p_hi, p_lo, p_lo], axis=1)
    v_hi, v_lo = halves(g_t[...])
    q_all = jnp.concatenate(halves(-g_p[...]), axis=1)
    load_v.wait()
    stores = []
    for step in range(rows // CHUNK):
        here = slice(step * CHUNK, step * CHUNK + CHUNK)
        tile = tile_u[here, :]
        out_u[here, :] = nt(tile, u_hi, None) + nt(tile, u_lo, None) + nt(up[here, :], p_all, None)
        tile = tile_v[here, :]
        stores.append(pltpu.make_async_copy(out_u.at[here, :], out_u_hbm.at[here, :], out_sem.at[0, step]))
        stores[-1].start()
        out_v[here, :] = nt(tile, v_hi, None) + nt(tile, v_lo, None) + nt(wide_u[here, :], q_all, None)
        stores.append(pltpu.make_async_copy(out_v.at[here, :], out_v_hbm.at[here, :], out_sem.at[1, step]))
        stores[-1].start()
    for store in stores:
        store.wait()


def main_call(ranks, y_t, x_t, y_p, tile_u, tile_v, mine, other, sides):
    rows = tile_u.shape[0]
    hbm = pl.BlockSpec(memory_space=pl.ANY)
    out = jax.ShapeDtypeStruct((rows, 256), F32)
    block = pltpu.VMEM((256, 256), F32)
    thin = pltpu.VMEM((256, 64), F32)
    wide = pltpu.VMEM((rows, 256), BF16)
    half = pltpu.VMEM((rows, 128), BF16)
    result = pltpu.VMEM((rows, 256), F32)
    return pl.pallas_call(
        main_kernel,
        out_shape=(out, out),
        in_specs=[pl.BlockSpec(memory_space=pltpu.SMEM)] + [hbm] * 17,
        out_specs=(hbm, hbm),
        scratch_shapes=[
            block, block, thin, wide, wide, pltpu.VMEM((2, rows, 256), BF16), half, wide, half, result, result,
            pltpu.VMEM((256, 512), F32), block, thin, block, thin,
            pltpu.SemaphoreType.DMA((29,)), pltpu.SemaphoreType.DMA((2, rows // CHUNK)),
        ],
        compiler_params=pltpu.CompilerParams(vmem_limit_bytes=VMEM_LIMIT),
        cost_estimate=pl.CostEstimate(flops=20 * 10**9, bytes_accessed=15 * 10**6, transcendentals=0),
        name="recompress",
    )(ranks, y_t, x_t, y_p, tile_u, tile_v, *mine, *other, *sides)


def send(x, axis, count, step):
    return lax.ppermute(x, axis, [(i, step(i)) for i in range(count)])


def body(tile_u, tile_v, row_u, row_v, col_u, col_v, tile_rank, row_rank, col_rank, target_rank, sketch):
    spot_i, spot_j = lax.axis_index("row"), lax.axis_index("col")
    core, x, y_low = spot_j % 2, spot_j // 2 % 4, spot_j // 8
    z, y_half = spot_i // 2, spot_i % 2
    first = core == 0
    own_u, own_v = tile_u[0, 0], tile_v[0, 0]
    numbers = [tile_rank[0, 0], row_rank[0], col_rank[0], target_rank[0, 0], core, y_low, z, x, y_half]
    ranks = jnp.stack(numbers).astype(jnp.int32)
    side = jnp.concatenate([col_u[0], col_v[0]], axis=1)
    side_other = send(side, "row", 8, lambda i: i ^ 1)
    give = jnp.where(first, row_v[0], row_u[0])
    keep = jnp.where(first, row_u[0], row_v[0])
    got = send(give, "col", 16, lambda i: i ^ 1)
    chip = jnp.concatenate([jnp.where(first, keep, got), jnp.where(first, got, keep)], axis=0)
    chip_other = send(chip, "col", 16, lambda i: i ^ 8)
    side_other, chip_other, own_u, own_v = lax.optimization_barrier((side_other, chip_other, own_u, own_v))
    sides = [jnp.stack([side, side_other])]
    mine = [jnp.stack([chip, chip_other])]
    for shift in SHIFTS[1:]:
        mine.append(send(mine[0], "col", 16, lambda i: i // 8 * 8 + (i + 2 * shift) % 8))
    for shift in SHIFTS[1:]:
        sides.append(send(sides[0], "row", 8, lambda i: (i + 2 * shift) % 8))
    low_inv, sketch_t, y_t, x_t = own_call(ranks, sketch, own_u, own_v)
    low_inv, mine, sides = lax.optimization_barrier((low_inv, mine, sides))
    other = [send(piece, "col", 16, lambda i: i ^ 1) for piece in mine]
    y_p = side_call(ranks, low_inv, sketch_t, own_v, sides)
    new_u, new_v = main_call(ranks, y_t, x_t, y_p, own_u, own_v, mine, other, sides)
    return (new_u[None, None], new_v[None, None])


def solution(mesh):
    placed = (
        P("row", "col", None, None),
        P("row", "col", None, None),
        P("row", "col", None),
        P("row", "col", None),
        P("col", "row", None),
        P("col", "row", None),
        P("row", "col"),
        P("row"),
        P("col"),
        P("row", "col"),
        P(),
    )
    return jax.shard_map(
        body,
        mesh=mesh,
        in_specs=placed,
        out_specs=(P("row", "col", None, None), P("row", "col", None, None)),
        check_vma=False,
    )
```

```python
import math

import jax
import jax.numpy as jnp
from jax import lax
from jax.experimental import pallas as pl
from jax.experimental.pallas import tpu as pltpu
from jax.sharding import PartitionSpec as P

F32 = jnp.float32
BF16 = jnp.bfloat16
HIGH = lax.Precision.HIGHEST
CHUNK = 896
TOLERANCE = 3e-4
VMEM_LIMIT = 60 * 1024 * 1024


def nn(a, b, precision=HIGH):
    return lax.dot_general(a, b, (((1,), (0,)), ((), ())), precision=precision, preferred_element_type=F32)


def nt(a, b, precision=HIGH):
    return lax.dot_general(a, b, (((1,), (1,)), ((), ())), precision=precision, preferred_element_type=F32)


def tn(a, b, precision=None):
    return lax.dot_general(a, b, (((0,), (0,)), ((), ())), precision=precision, preferred_element_type=F32)


def lane_splat(x, lane):
    return jnp.broadcast_to(x[:, lane : lane + 1], x.shape)


def row_splat(x, row):
    return jnp.broadcast_to(x[row : row + 1, :], x.shape)


def total(terms):
    while len(terms) > 1:
        terms = [terms[k] + terms[k + 1] if k + 1 < len(terms) else terms[k] for k in range(0, len(terms), 2)]
    return terms[0]


def leaf(block):
    count = 8
    rows = [block[8 * r : 8 * r + 8, :] for r in range(count)]
    sub = lax.broadcasted_iota(jnp.int32, (8, 128), 0)
    diag = [lane_splat(rows[0], 64 + m) for m in range(8)]
    for b in range(count):
        more = b + 1 < count
        x = rows[b]
        if more:
            ahead = rows[b + 1]
            side = [lane_splat(ahead, 64 + 8 * b + m) for m in range(8)]
            following = [lane_splat(ahead, 72 + 8 * b + m) for m in range(8)]
        far = {r: [lane_splat(rows[r], 64 + 8 * b + m) for m in range(8)] for r in range(b + 2, count)}
        inverse, pivot_rows, low = [], [], []
        pivots = diag[0]
        for k in range(8):
            r = 1.0 / row_splat(diag[k], k)
            inverse.append(r)
            if k:
                pivots = jnp.where(sub == k, diag[k], pivots)
            below = jnp.where(sub > k, diag[k], 0.0)
            low.append(below)
            pivot = row_splat(x, k) * r
            pivot_rows.append(pivot)
            for m in range(k + 1, 8):
                entry = row_splat(diag[m], k)
                diag[m] = diag[m] - (below * entry) * r
                if more:
                    side[m] = side[m] - side[k] * (entry * r)
            x = x - below * pivot
            if more:
                ahead = ahead - side[k] * pivot
        if more:
            scaled = [side[k] * inverse[k] for k in range(8)]
            diag = [
                following[m] - total([scaled[k] * row_splat(side[k], m) for k in range(8)]) for m in range(8)
            ]
            rows[b + 1] = ahead
        if far:
            back = [None] * 8
            for k in range(7, -1, -1):
                column = low[k] * inverse[k]
                back[k] = pivot_rows[k]
                for i in range(k + 1, 8):
                    back[k] = back[k] - row_splat(column, i) * back[i]
            for r in far:
                rows[r] = rows[r] - total([far[r][m] * back[m] for m in range(8)])
        rows[b] = x * lax.rsqrt(pivots)
    return jnp.concatenate(rows, axis=0)


def shifted(pair):
    lane = lax.broadcasted_iota(jnp.int32, pair.shape, 1)
    return jnp.where(lane >= 64, pltpu.roll(pair, 64, 1), 0.0)


def spread(matrix, aug_ref):
    size = matrix.shape[0]
    lane = lax.broadcasted_iota(jnp.int32, (size, 128), 1)
    row = lax.broadcasted_iota(jnp.int32, (size, 128), 0)
    for k in range(size // 64):
        half = matrix[:, 128 * (k // 2) : 128 * (k // 2) + 128]
        if k % 2 == 0:
            half = pltpu.roll(half, 64, 1)
        eye = (row == lane + 64 * k).astype(F32)
        aug_ref[:, 128 * k : 128 * k + 128] = jnp.where(lane >= 64, half, eye)


def gather_inverse(aug_ref):
    lane = lax.broadcasted_iota(jnp.int32, (aug_ref.shape[0], 128), 1)
    parts = []
    for t in range(aug_ref.shape[1] // 256):
        even = aug_ref[:, 256 * t : 256 * t + 128]
        odd = aug_ref[:, 256 * t + 128 : 256 * t + 256]
        parts.append(jnp.where(lane < 64, even, pltpu.roll(odd, 64, 1)))
    return jnp.concatenate(parts, axis=1)


def factor(aug_ref, low_refs=None, begin=0, end=None, start=None):
    size = aug_ref.shape[0]
    count = size // 64
    if start is None:
        start = aug_ref[:64, :128]
    for k in range(begin, count if end is None else end):
        here = slice(64 * k, 64 * k + 64)
        tile = slice(128 * k, 128 * k + 128)
        pair = leaf(start)
        wide = shifted(pair)
        inverse = pair[:, :64]
        if low_refs is not None:
            low_refs[k][here, :] = nt(start, wide)
        if k + 1 == count:
            aug_ref[here, :] = nn(inverse, aug_ref[here, :])
            break
        below = slice(64 * k + 64, 64 * k + 128)
        after = slice(128 * k + 128, 128 * k + 256)
        near = nt(aug_ref[below, tile], wide)
        start = aug_ref[below, after] - nn(near, nn(inverse, aug_ref[here, after]))
        ahead = nn(inverse, aug_ref[here, :])
        left = nt(aug_ref[64 * k + 64 :, tile], wide)
        aug_ref[here, :] = ahead
        if low_refs is not None:
            low_refs[k][64 * k + 64 :, :] = left
        aug_ref[64 * k + 64 :, :] = aug_ref[64 * k + 64 :, :] - nn(left, ahead)
    return start


def masked_gram(gram, rank):
    size = gram.shape[0]
    row = lax.broadcasted_iota(jnp.int32, gram.shape, 0)
    col = lax.broadcasted_iota(jnp.int32, gram.shape, 1)
    both = (row < rank) & (col < rank)
    dead = (row == col) & (row >= rank)
    return jnp.where(both, gram, 0.0), dead.astype(F32)


def iota(shape, dim):
    return lax.broadcasted_iota(jnp.int32, shape, dim)


def halves(x):
    top = x.astype(BF16)
    return top, (x - top.astype(F32)).astype(BF16)


def lower_only(x):
    return jnp.where(iota(x.shape, 0) >= iota(x.shape, 1), x, 0.0)


def places():
    spot_i, spot_j = lax.axis_index("row"), lax.axis_index("col")
    return lax.rem(spot_j, 2), spot_j // 8, spot_i // 2, lax.rem(spot_j // 2, 4), lax.rem(spot_i, 2)


def copy_all(pairs, sem):
    copies = [pltpu.make_async_copy(source, target, sem.at[k]) for k, (source, target) in enumerate(pairs)]
    for copy in copies:
        copy.start()
    return copies


def early_kernel(
    rank_t, sketch_hbm, tile_u_hbm, tile_v_hbm,
    gram_hbm, sketch_t_hbm, aug_hbm, low0_hbm,
    sketch, tile_u, tile_v, gram, sketch_t, aug_ref, low0, in_sem, out_sem
):
    loads = copy_all([(tile_v_hbm, tile_v), (tile_u_hbm, tile_u), (sketch_hbm, sketch)], in_sem)
    rank = rank_t[0, 0]
    loads[0].wait()
    gram_v, dead = masked_gram(tn(tile_v[...], tile_v[...]), rank)
    spread(gram_v + dead, aug_ref)
    loads[1].wait()
    loads[2].wait()
    gram[...] = masked_gram(tn(tile_u[...], tile_u[...]), rank)[0]
    flipped = sketch[...].T
    sketch_t[...] = flipped
    factor(aug_ref, (low0,), 0, 1)
    pairs = [(gram, gram_hbm), (sketch_t, sketch_t_hbm), (aug_ref, aug_hbm), (low0, low0_hbm)]
    for store in copy_all(pairs, out_sem):
        store.wait()


def early_call(rank, sketch, tile_u, tile_v):
    wide = pltpu.VMEM(tile_u.shape, BF16)
    hbm = pl.BlockSpec(memory_space=pl.ANY)
    shapes = [(256, 256), (256, 320), (256, 512), (256, 64)]
    return pl.pallas_call(
        early_kernel,
        out_shape=[jax.ShapeDtypeStruct(shape, F32) for shape in shapes],
        in_specs=[pl.BlockSpec(memory_space=pltpu.SMEM)] + [hbm] * 3,
        out_specs=[hbm] * 4,
        scratch_shapes=[pltpu.VMEM((320, 256), F32), wide, wide]
        + [pltpu.VMEM(shape, F32) for shape in shapes]
        + [pltpu.SemaphoreType.DMA((3,)), pltpu.SemaphoreType.DMA((4,))],
        compiler_params=pltpu.CompilerParams(vmem_limit_bytes=VMEM_LIMIT),
        cost_estimate=pl.CostEstimate(flops=7 * 10**9, bytes_accessed=4 * 10**6, transcendentals=0),
        name="early_factor",
    )(rank, sketch, tile_u, tile_v)


def middle_kernel(aug_hbm, aug_out_hbm, low1_hbm, low2_hbm, aug_ref, low1, low2, in_sem, out_sem):
    load = pltpu.make_async_copy(aug_hbm, aug_ref, in_sem)
    load.start()
    low1[:64, :] = jnp.zeros((64, 64), F32)
    low2[:128, :] = jnp.zeros((128, 64), F32)
    load.wait()
    factor(aug_ref, (None, low1, low2), 1, 3, aug_ref[64:128, 128:256])
    for store in copy_all([(aug_ref, aug_out_hbm), (low1, low1_hbm), (low2, low2_hbm)], out_sem):
        store.wait()


def middle_call(aug):
    hbm = pl.BlockSpec(memory_space=pl.ANY)
    shapes = [(256, 512), (256, 64), (256, 64)]
    return pl.pallas_call(
        middle_kernel,
        out_shape=[jax.ShapeDtypeStruct(shape, F32) for shape in shapes],
        in_specs=[hbm],
        out_specs=[hbm] * 3,
        scratch_shapes=[pltpu.VMEM(shape, F32) for shape in shapes] + [pltpu.SemaphoreType.DMA, pltpu.SemaphoreType.DMA((3,))],
        compiler_params=pltpu.CompilerParams(vmem_limit_bytes=VMEM_LIMIT),
        cost_estimate=pl.CostEstimate(flops=6 * 10**9, bytes_accessed=2 * 10**6, transcendentals=0),
        name="middle_factor",
    )(aug)


def late_kernel(
    rank_t, aug_hbm, low0_hbm, low1_hbm, low2_hbm, sketch_t_hbm, gram_hbm,
    low_inv_hbm, y_hbm, x_hbm,
    aug_ref, low0, low1, low2, sketch_t, gram, low3, low_inv, y_ref, x_ref, in_sem, out_sem,
):
    pairs = [(aug_hbm, aug_ref), (low0_hbm, low0), (low1_hbm, low1), (low2_hbm, low2), (sketch_t_hbm, sketch_t), (gram_hbm, gram)]
    loads = copy_all(pairs, in_sem)
    low3[:192, :] = jnp.zeros((192, 64), F32)
    for load in loads:
        load.wait()
    lows = (low0, low1, low2, low3)
    factor(aug_ref, lows, 3, 4, aug_ref[192:256, 384:512])
    low_inv[...] = gather_inverse(aug_ref)
    low = lower_only(jnp.concatenate([ref[...] for ref in lows], axis=1))
    y = jnp.where(iota((256, 256), 1) < rank_t[0, 0], nt(sketch_t[:, :256], low), 0.0)
    y_ref[...] = y
    x_ref[...] = nn(y, gram[...])
    for store in copy_all([(low_inv, low_inv_hbm), (y_ref, y_hbm), (x_ref, x_hbm)], out_sem):
        store.wait()


def late_call(rank, aug, low0, low1, low2, sketch_t, gram):
    hbm = pl.BlockSpec(memory_space=pl.ANY)
    square = jax.ShapeDtypeStruct((256, 256), F32)
    block, thin = pltpu.VMEM((256, 256), F32), pltpu.VMEM((256, 64), F32)
    return pl.pallas_call(
        late_kernel,
        out_shape=[square] * 3,
        in_specs=[pl.BlockSpec(memory_space=pltpu.SMEM)] + [hbm] * 6,
        out_specs=[hbm] * 3,
        scratch_shapes=[pltpu.VMEM((256, 512), F32), thin, thin, thin, pltpu.VMEM((256, 320), F32), block, thin, block, block, block]
        + [pltpu.SemaphoreType.DMA((6,)), pltpu.SemaphoreType.DMA((3,))],
        compiler_params=pltpu.CompilerParams(vmem_limit_bytes=VMEM_LIMIT),
        cost_estimate=pl.CostEstimate(flops=6 * 10**9, bytes_accessed=2 * 10**6, transcendentals=0),
        name="late_factor",
    )(rank, aug, low0, low1, low2, sketch_t, gram)


def panel_copies(pieces, target, sem):
    core, y_low, z, x, y_half = places()
    block = pieces[0].shape[1]
    left, right = lax.rem(x + 3, 4), lax.rem(x + 1, 4)
    come, back = jnp.where(core == 0, left, right), jnp.where(core == 0, right, left)
    across = lax.rem(x + 2, 4)
    other = 1 - core
    spots = [
        (core, x), (other, x), (core, come), (other, come),
        (other, back), (core, back), (core, across), (other, across),
    ]
    copies = []
    for array, (slot, place) in zip(pieces, spots):
        for k in range(2):
            start = (lax.rem(y_low + k, 2) * 4 + place) * block
            spot = pl.ds(pl.multiple_of(start, block), block)
            copies.append(pltpu.make_async_copy(array.at[k], target.at[slot, spot, :], sem.at[len(copies)]))
    return copies


def side_copies(own, near, swapped, far, target, sem):
    core, y_low, z, x, y_half = places()
    block = own.shape[1]
    down, up = lax.rem(z + 3, 4), lax.rem(z + 1, 4)
    come, back = jnp.where(core == 0, down, up), jnp.where(core == 0, up, down)
    copies = []
    for array, place in ((own, z), (near, come), (swapped, back), (far, lax.rem(z + 2, 4))):
        for k in range(2):
            start = (place * 2 + lax.rem(y_half + k, 2)) * block
            spot = pl.ds(pl.multiple_of(start, block), block)
            copies.append(pltpu.make_async_copy(array.at[k], target.at[spot, :], sem.at[16 + len(copies)]))
    return copies


def main_kernel(
    rank_t, rank_i, rank_j, rank_s, low_inv_hbm, sketch_t_hbm, y_t_hbm, x_t_hbm, tile_u_hbm, tile_v_hbm,
    row0, row1, row2, row3, row4, row5, row6, row7, side_own, side_near, side_swapped, side_far,
    out_u_hbm, out_v_hbm,
    low_inv, sketch_t, y_t, x_t, tile_u, tile_v, panel, col_uv, up, wide_u, out_u, out_v, aug_ref, w_t, g_t, p_ref,
    in_sem, out_sem
):
    rows = tile_u.shape[0]
    t_rank, i_rank, j_rank, s_rank = rank_t[0, 0], rank_i[0], rank_j[0], rank_s[0, 0]
    arrived = side_copies(side_own, side_near, side_swapped, side_far, col_uv, in_sem)
    arrived += panel_copies((row0, row1, row2, row3, row4, row5, row6, row7), panel, in_sem)
    pairs = [
        (tile_v_hbm, tile_v), (low_inv_hbm, low_inv), (sketch_t_hbm, sketch_t),
        (y_t_hbm, y_t), (x_t_hbm, x_t), (tile_u_hbm, tile_u),
    ]
    kept = [pltpu.make_async_copy(source, target, in_sem.at[24 + k]) for k, (source, target) in enumerate(pairs)]
    for load in arrived + kept:
        load.start()
    for load in arrived:
        load.wait()
    sides = col_uv[...]
    keep = (iota((64, 256), 0) < j_rank) & (iota((64, 256), 1) < i_rank)
    cross_t = jnp.where(keep, tn(sides, panel[1])[64:], 0.0).astype(BF16)
    for load in kept:
        load.wait()
    keep = (iota((64, 256), 0) < j_rank) & (iota((64, 256), 1) < t_rank)
    side = jnp.where(keep, -tn(sides, tile_v[...])[:64], 0.0)
    corner, dead = masked_gram(tn(sides, sides)[:64, :64], j_rank)
    low_pt = nt(side, low_inv[...])
    schur = corner + dead - nt(low_pt, low_pt)
    eye = (iota((64, 64), 0) == iota((64, 64), 1)).astype(F32)
    start = jnp.concatenate([eye, schur], axis=1)
    low_pp = lower_only(nt(start, shifted(leaf(start))))
    for step in range(rows // CHUNK):
        here = slice(step * CHUNK, step * CHUNK + CHUNK)
        top, rest = halves(nt(panel[0, here, :], cross_t, None))
        up[here, :] = jnp.concatenate([top, rest, top, rest], axis=1)
        part = col_uv[here, :][:, :64]
        wide_u[here, :] = jnp.concatenate([part, part], axis=1)
    both = tn(up[:, :128], tile_u[...])
    gram_pt = jnp.where(keep, both[:64] + both[64:], 0.0)
    four = tn(up[:, :128], up[:, :128])
    four = four[:64] + four[64:]
    gram_pp = (four + pltpu.roll(four, 64, 1))[:, :64]
    drawn = iota((256, 256), 0) < s_rank
    ys = jnp.where(drawn, y_t[...], 0.0)
    yp = nt(sketch_t[:, :256], low_pt) + nt(sketch_t[:, 256:], low_pp)
    yp = jnp.where((iota((256, 64), 1) < j_rank) & (iota((256, 64), 0) < s_rank), yp, 0.0)
    xs = jnp.where(drawn, x_t[...], 0.0) + nn(yp, gram_pt)
    xp = nt(ys, gram_pt) + nn(yp, gram_pp)
    same = iota((256, 256), 0) == iota((256, 256), 1)
    dead = (same & (iota((256, 256), 0) >= s_rank)).astype(F32)
    spread(nt(xs, ys) + nt(xp, yp) + dead, aug_ref)
    factor(aug_ref)
    inverse = gather_inverse(aug_ref)
    w_t[...] = nn(inverse, ys)
    g_t[...] = nn(inverse, xs)
    p_ref[...] = nn(inverse, jnp.concatenate([yp, xp], axis=1))
    live = (same & (iota((256, 256), 0) < s_rank)).astype(F32)

    def refine(state):
        count, unused = state
        pair = p_ref[...]
        upper = jnp.where(iota(pair.shape, 1) < 64, pair, 0.0)
        error = nt(w_t[...], g_t[...]) + nt(upper, pltpu.roll(pair, 64, 1)) - live
        size = jnp.max(jnp.sum(jnp.abs(error), axis=1, keepdims=True))
        step = (lower_only(error) - jnp.where(same, 0.5 * error, 0.0)).astype(BF16)
        for ref in (w_t, g_t, p_ref):
            ref[...] = ref[...] - nn(step, ref[...].astype(BF16), None)
        return count + 1, size

    lax.while_loop(lambda s: (s[0] < 12) & (s[1] > TOLERANCE), refine, (jnp.int32(0), jnp.float32(1.0)))
    scale = math.sqrt(rows)
    u_hi, u_lo = halves(w_t[...] * scale)
    pair = p_ref[...]
    p_hi, p_lo = halves(pair[:, :64] * scale)
    v_hi, v_lo = halves(g_t[...])
    u_all = jnp.concatenate([u_hi, u_lo, p_hi, p_hi, p_lo, p_lo], axis=1)
    v_all = jnp.concatenate([v_hi, v_lo, *halves(-pair[:, 64:])], axis=1)
    stores = []
    for step in range(rows // CHUNK):
        here = slice(step * CHUNK, step * CHUNK + CHUNK)
        tile = tile_u[here, :]
        out_u[here, :] = nt(jnp.concatenate([tile, tile, up[here, :]], axis=1), u_all, None)
        tile = tile_v[here, :]
        stores.append(pltpu.make_async_copy(out_u.at[here, :], out_u_hbm.at[here, :], out_sem.at[0, step]))
        stores[-1].start()
        out_v[here, :] = nt(jnp.concatenate([tile, tile, wide_u[here, :]], axis=1), v_all, None)
        stores.append(pltpu.make_async_copy(out_v.at[here, :], out_v_hbm.at[here, :], out_sem.at[1, step]))
        stores[-1].start()
    for store in stores:
        store.wait()


def main_call(ranks, low_inv, sketch_t, y_t, x_t, tile_u, tile_v, panels, sides):
    rows = tile_u.shape[0]
    hbm = pl.BlockSpec(memory_space=pl.ANY)
    out = jax.ShapeDtypeStruct((rows, 256), F32)
    block = pltpu.VMEM((256, 256), F32)
    wide = pltpu.VMEM((rows, 256), BF16)
    half = pltpu.VMEM((rows, 128), BF16)
    result = pltpu.VMEM((rows, 256), F32)
    return pl.pallas_call(
        main_kernel,
        out_shape=(out, out),
        in_specs=[pl.BlockSpec(memory_space=pltpu.SMEM)] * 4 + [hbm] * 18,
        out_specs=(hbm, hbm),
        scratch_shapes=[
            block, pltpu.VMEM((256, 320), F32), block, block, wide, wide, pltpu.VMEM((2, rows, 256), BF16), half, wide, half, result, result,
            pltpu.VMEM((256, 512), F32), block, block, pltpu.VMEM((256, 128), F32),
            pltpu.SemaphoreType.DMA((30,)), pltpu.SemaphoreType.DMA((2, rows // CHUNK)),
        ],
        compiler_params=pltpu.CompilerParams(vmem_limit_bytes=VMEM_LIMIT),
        cost_estimate=pl.CostEstimate(flops=20 * 10**9, bytes_accessed=15 * 10**6, transcendentals=0),
        name="recompress",
    )(*ranks, low_inv, sketch_t, y_t, x_t, tile_u, tile_v, *panels, *sides)


def send(x, axis, count, step):
    return lax.ppermute(x, axis, [(i, step(i)) for i in range(count)])


def swap(x):
    return send(x, "col", 16, lambda i: i ^ 1)


def round_x(x):
    return send(x, "col", 16, lambda i: i // 8 * 8 + (i + (2 if i % 2 == 0 else 6)) % 8)


def round_z(x):
    return send(x, ("row", "col"), 128, lambda i: (i + (32 if i % 2 == 0 else 96)) % 128)


def body(tile_u, tile_v, row_u, row_v, col_u, col_v, tile_rank, row_rank, col_rank, target_rank, sketch):
    first = lax.axis_index("col") % 2 == 0
    own_u, own_v = tile_u[0, 0], tile_v[0, 0]
    side = jnp.concatenate([col_u[0], col_v[0]], axis=1)
    give = jnp.where(first, row_v[0], row_u[0])
    keep = jnp.where(first, row_u[0], row_v[0])
    got = swap(give)
    chip = jnp.concatenate([jnp.where(first, keep, got), jnp.where(first, got, keep)], axis=0)
    chip, side = lax.optimization_barrier((chip, side))
    chip_other = send(chip, "col", 16, lambda i: i ^ 8)
    side_other = send(side, "row", 8, lambda i: i ^ 1)
    chip_swapped, side_swapped = swap(chip), swap(side)
    early = early_call(tile_rank, sketch, own_u, own_v)
    early, side_other, chip_other, chip_swapped, side_swapped = lax.optimization_barrier(
        (early, side_other, chip_other, chip_swapped, side_swapped)
    )
    gram, sketch_t, aug, low0 = early
    mine = jnp.stack([chip, chip_other])
    side_all = jnp.stack([side, side_other, side_swapped, swap(side_other)])
    near = round_x(mine)
    theirs = jnp.stack([chip_swapped, swap(chip_other)])
    near_theirs = round_x(theirs)
    side_near = round_z(side_all)
    aug, low1, low2 = middle_call(aug)
    aug, near, side_near = lax.optimization_barrier((aug, near, side_near))
    far, side_far = round_x(near), round_z(side_near[:2])
    near_swapped, side_back = swap(near), swap(side_near[2:])
    low_inv, y_t, x_t = late_call(tile_rank, aug, low0, low1, low2, sketch_t, gram)
    theirs_swapped = swap(near_theirs)
    far, side_far, near_swapped, side_back, theirs_swapped, y_t, row_rank, col_rank, target_rank = lax.optimization_barrier(
        (far, side_far, near_swapped, side_back, theirs_swapped, y_t, row_rank, col_rank, target_rank)
    )
    ranks = (tile_rank, row_rank, col_rank, target_rank)
    panels = [mine, theirs, near, near_theirs, near_swapped, theirs_swapped, far, swap(far)]
    sides = [side_all, side_near, side_back, side_far]
    new_u, new_v = main_call(ranks, low_inv, sketch_t, y_t, x_t, own_u, own_v, panels, sides)
    return (new_u[None, None], new_v[None, None])


def solution(mesh):
    placed = (
        P("row", "col", None, None),
        P("row", "col", None, None),
        P("row", "col", None),
        P("row", "col", None),
        P("col", "row", None),
        P("col", "row", None),
        P("row", "col"),
        P("row"),
        P("col"),
        P("row", "col"),
        P(),
    )
    return jax.shard_map(
        body,
        mesh=mesh,
        in_specs=placed,
        out_specs=(P("row", "col", None, None), P("row", "col", None, None)),
        check_vma=False,
    )
```

```python
import math

import jax
import jax.numpy as jnp
from jax import lax
from jax.experimental import pallas as pl
from jax.experimental.pallas import tpu as pltpu
from jax.sharding import PartitionSpec as P

F32 = jnp.float32
BF16 = jnp.bfloat16
HIGH = lax.Precision.HIGHEST
CHUNK = 896
TOLERANCE = 3e-4
VMEM_LIMIT = 60 * 1024 * 1024


def nn(a, b, precision=HIGH):
    return lax.dot_general(a, b, (((1,), (0,)), ((), ())), precision=precision, preferred_element_type=F32)


def nt(a, b, precision=HIGH):
    return lax.dot_general(a, b, (((1,), (1,)), ((), ())), precision=precision, preferred_element_type=F32)


def tn(a, b, precision=None):
    return lax.dot_general(a, b, (((0,), (0,)), ((), ())), precision=precision, preferred_element_type=F32)


def lane_splat(x, lane):
    return jnp.broadcast_to(x[:, lane : lane + 1], x.shape)


def row_splat(x, row):
    return jnp.broadcast_to(x[row : row + 1, :], x.shape)


def total(terms):
    while len(terms) > 1:
        terms = [terms[k] + terms[k + 1] if k + 1 < len(terms) else terms[k] for k in range(0, len(terms), 2)]
    return terms[0]


def leaf(block):
    count = 8
    rows = [block[8 * r : 8 * r + 8, :] for r in range(count)]
    sub = lax.broadcasted_iota(jnp.int32, (8, 128), 0)
    diag = [lane_splat(rows[0], 64 + m) for m in range(8)]
    for b in range(count):
        more = b + 1 < count
        x = rows[b]
        if more:
            ahead = rows[b + 1]
            side = [lane_splat(ahead, 64 + 8 * b + m) for m in range(8)]
            following = [lane_splat(ahead, 72 + 8 * b + m) for m in range(8)]
        far = {r: [lane_splat(rows[r], 64 + 8 * b + m) for m in range(8)] for r in range(b + 2, count)}
        inverse, pivot_rows, low = [], [], []
        pivots = diag[0]
        for k in range(8):
            r = 1.0 / row_splat(diag[k], k)
            inverse.append(r)
            if k:
                pivots = jnp.where(sub == k, diag[k], pivots)
            below = jnp.where(sub > k, diag[k], 0.0)
            low.append(below)
            pivot = row_splat(x, k) * r
            pivot_rows.append(pivot)
            for m in range(k + 1, 8):
                entry = row_splat(diag[m], k)
                diag[m] = diag[m] - (below * entry) * r
                if more:
                    side[m] = side[m] - side[k] * (entry * r)
            x = x - below * pivot
            if more:
                ahead = ahead - side[k] * pivot
        if more:
            scaled = [side[k] * inverse[k] for k in range(8)]
            diag = [
                following[m] - total([scaled[k] * row_splat(side[k], m) for k in range(8)]) for m in range(8)
            ]
            rows[b + 1] = ahead
        if far:
            back = [None] * 8
            for k in range(7, -1, -1):
                column = low[k] * inverse[k]
                back[k] = pivot_rows[k]
                for i in range(k + 1, 8):
                    back[k] = back[k] - row_splat(column, i) * back[i]
            for r in far:
                rows[r] = rows[r] - total([far[r][m] * back[m] for m in range(8)])
        rows[b] = x * lax.rsqrt(pivots)
    return jnp.concatenate(rows, axis=0)


def shifted(pair):
    lane = lax.broadcasted_iota(jnp.int32, pair.shape, 1)
    return jnp.where(lane >= 64, pltpu.roll(pair, 64, 1), 0.0)


def spread(matrix, aug_ref):
    size = matrix.shape[0]
    lane = lax.broadcasted_iota(jnp.int32, (size, 128), 1)
    row = lax.broadcasted_iota(jnp.int32, (size, 128), 0)
    for k in range(size // 64):
        half = matrix[:, 128 * (k // 2) : 128 * (k // 2) + 128]
        if k % 2 == 0:
            half = pltpu.roll(half, 64, 1)
        eye = (row == lane + 64 * k).astype(F32)
        aug_ref[:, 128 * k : 128 * k + 128] = jnp.where(lane >= 64, half, eye)


def gather_inverse(aug_ref):
    lane = lax.broadcasted_iota(jnp.int32, (aug_ref.shape[0], 128), 1)
    parts = []
    for t in range(aug_ref.shape[1] // 256):
        even = aug_ref[:, 256 * t : 256 * t + 128]
        odd = aug_ref[:, 256 * t + 128 : 256 * t + 256]
        parts.append(jnp.where(lane < 64, even, pltpu.roll(odd, 64, 1)))
    return jnp.concatenate(parts, axis=1)


def factor(aug_ref, low_refs=None, begin=0, end=None, start=None):
    size = aug_ref.shape[0]
    count = size // 64
    if start is None:
        start = aug_ref[:64, :128]
    for k in range(begin, count if end is None else end):
        here = slice(64 * k, 64 * k + 64)
        tile = slice(128 * k, 128 * k + 128)
        pair = leaf(start)
        wide = shifted(pair)
        inverse = pair[:, :64]
        if low_refs is not None:
            low_refs[k][here, :] = nt(start, wide)
        if k + 1 == count:
            aug_ref[here, :] = nn(inverse, aug_ref[here, :])
            break
        below = slice(64 * k + 64, 64 * k + 128)
        after = slice(128 * k + 128, 128 * k + 256)
        near = nt(aug_ref[below, tile], wide)
        start = aug_ref[below, after] - nn(near, nn(inverse, aug_ref[here, after]))
        ahead = nn(inverse, aug_ref[here, :])
        left = nt(aug_ref[64 * k + 64 :, tile], wide)
        aug_ref[here, :] = ahead
        if low_refs is not None:
            low_refs[k][64 * k + 64 :, :] = left
        aug_ref[64 * k + 64 :, :] = aug_ref[64 * k + 64 :, :] - nn(left, ahead)
    return start


def masked_gram(gram, rank):
    size = gram.shape[0]
    row = lax.broadcasted_iota(jnp.int32, gram.shape, 0)
    col = lax.broadcasted_iota(jnp.int32, gram.shape, 1)
    both = (row < rank) & (col < rank)
    dead = (row == col) & (row >= rank)
    return jnp.where(both, gram, 0.0), dead.astype(F32)


def iota(shape, dim):
    return lax.broadcasted_iota(jnp.int32, shape, dim)


def halves(x):
    top = x.astype(BF16)
    return top, (x - top.astype(F32)).astype(BF16)


def lower_only(x):
    return jnp.where(iota(x.shape, 0) >= iota(x.shape, 1), x, 0.0)


def places():
    spot_i, spot_j = lax.axis_index("row"), lax.axis_index("col")
    return lax.rem(spot_j, 2), spot_j // 8, spot_i // 2, lax.rem(spot_j // 2, 4), lax.rem(spot_i, 2)


def copy_all(pairs, sem):
    copies = [pltpu.make_async_copy(source, target, sem.at[k]) for k, (source, target) in enumerate(pairs)]
    for copy in copies:
        copy.start()
    return copies


def early_kernel(
    rank_t, sketch_hbm, tile_u_hbm, tile_v_hbm,
    gram_hbm, sketch_t_hbm, aug_hbm, low0_hbm,
    sketch, tile_u, tile_v, gram, sketch_t, aug_ref, low0, in_sem, out_sem
):
    loads = copy_all([(tile_v_hbm, tile_v), (tile_u_hbm, tile_u), (sketch_hbm, sketch)], in_sem)
    rank = rank_t[0, 0]
    loads[0].wait()
    gram_v, dead = masked_gram(tn(tile_v[...], tile_v[...]), rank)
    spread(gram_v + dead, aug_ref)
    loads[1].wait()
    loads[2].wait()
    flipped = sketch[...].T
    sketch_t[...] = flipped
    gram[...] = masked_gram(tn(tile_u[...], tile_u[...]), rank)[0]
    stores = [
        pltpu.make_async_copy(source, target, out_sem.at[k])
        for k, (source, target) in enumerate([(gram, gram_hbm), (sketch_t, sketch_t_hbm), (low0, low0_hbm), (aug_ref, aug_hbm)])
    ]
    stores[0].start()
    stores[1].start()
    factor(aug_ref, (low0,), 0, 1)
    stores[2].start()
    stores[3].start()
    for store in stores:
        store.wait()


def early_call(rank, sketch, tile_u, tile_v):
    wide = pltpu.VMEM(tile_u.shape, BF16)
    hbm = pl.BlockSpec(memory_space=pl.ANY)
    shapes = [(256, 256), (256, 320), (256, 512), (256, 64)]
    return pl.pallas_call(
        early_kernel,
        out_shape=[jax.ShapeDtypeStruct(shape, F32) for shape in shapes],
        in_specs=[pl.BlockSpec(memory_space=pltpu.SMEM)] + [hbm] * 3,
        out_specs=[hbm] * 4,
        scratch_shapes=[pltpu.VMEM((320, 256), F32), wide, wide]
        + [pltpu.VMEM(shape, F32) for shape in shapes]
        + [pltpu.SemaphoreType.DMA((3,)), pltpu.SemaphoreType.DMA((4,))],
        compiler_params=pltpu.CompilerParams(vmem_limit_bytes=VMEM_LIMIT),
        cost_estimate=pl.CostEstimate(flops=7 * 10**9, bytes_accessed=4 * 10**6, transcendentals=0),
        name="early_factor",
    )(rank, sketch, tile_u, tile_v)


def middle_kernel(aug_hbm, aug_out_hbm, low1_hbm, low2_hbm, aug_ref, low1, low2, in_sem, out_sem):
    load = pltpu.make_async_copy(aug_hbm, aug_ref, in_sem)
    load.start()
    low1[:64, :] = jnp.zeros((64, 64), F32)
    low2[:128, :] = jnp.zeros((128, 64), F32)
    load.wait()
    factor(aug_ref, (None, low1, low2), 1, 3, aug_ref[64:128, 128:256])
    for store in copy_all([(aug_ref, aug_out_hbm), (low1, low1_hbm), (low2, low2_hbm)], out_sem):
        store.wait()


def middle_call(aug):
    hbm = pl.BlockSpec(memory_space=pl.ANY)
    shapes = [(256, 512), (256, 64), (256, 64)]
    return pl.pallas_call(
        middle_kernel,
        out_shape=[jax.ShapeDtypeStruct(shape, F32) for shape in shapes],
        in_specs=[hbm],
        out_specs=[hbm] * 3,
        scratch_shapes=[pltpu.VMEM(shape, F32) for shape in shapes] + [pltpu.SemaphoreType.DMA, pltpu.SemaphoreType.DMA((3,))],
        compiler_params=pltpu.CompilerParams(vmem_limit_bytes=VMEM_LIMIT),
        cost_estimate=pl.CostEstimate(flops=6 * 10**9, bytes_accessed=2 * 10**6, transcendentals=0),
        name="middle_factor",
    )(aug)


def late_kernel(
    rank_t, aug_hbm, low0_hbm, low1_hbm, low2_hbm, sketch_t_hbm, gram_hbm,
    low_inv_hbm, y_hbm, x_hbm,
    aug_ref, low0, low1, low2, sketch_t, gram, low3, low_inv, y_ref, x_ref, in_sem, out_sem,
):
    pairs = [(aug_hbm, aug_ref), (low0_hbm, low0), (low1_hbm, low1), (low2_hbm, low2), (sketch_t_hbm, sketch_t), (gram_hbm, gram)]
    loads = copy_all(pairs, in_sem)
    low3[:192, :] = jnp.zeros((192, 64), F32)
    loads[0].wait()
    lows = (low0, low1, low2, low3)
    factor(aug_ref, lows, 3, 4, aug_ref[192:256, 384:512])
    low_inv[...] = gather_inverse(aug_ref)
    for load in loads[1:]:
        load.wait()
    low = lower_only(jnp.concatenate([ref[...] for ref in lows], axis=1))
    y = jnp.where(iota((256, 256), 1) < rank_t[0, 0], nt(sketch_t[:, :256], low), 0.0)
    y_ref[...] = y
    x_ref[...] = nn(y, gram[...])
    for store in copy_all([(low_inv, low_inv_hbm), (y_ref, y_hbm), (x_ref, x_hbm)], out_sem):
        store.wait()


def late_call(rank, aug, low0, low1, low2, sketch_t, gram):
    hbm = pl.BlockSpec(memory_space=pl.ANY)
    square = jax.ShapeDtypeStruct((256, 256), F32)
    block, thin = pltpu.VMEM((256, 256), F32), pltpu.VMEM((256, 64), F32)
    return pl.pallas_call(
        late_kernel,
        out_shape=[square] * 3,
        in_specs=[pl.BlockSpec(memory_space=pltpu.SMEM)] + [hbm] * 6,
        out_specs=[hbm] * 3,
        scratch_shapes=[pltpu.VMEM((256, 512), F32), thin, thin, thin, pltpu.VMEM((256, 320), F32), block, thin, block, block, block]
        + [pltpu.SemaphoreType.DMA((6,)), pltpu.SemaphoreType.DMA((3,))],
        compiler_params=pltpu.CompilerParams(vmem_limit_bytes=VMEM_LIMIT),
        cost_estimate=pl.CostEstimate(flops=6 * 10**9, bytes_accessed=2 * 10**6, transcendentals=0),
        name="late_factor",
    )(rank, aug, low0, low1, low2, sketch_t, gram)


def panel_copies(pieces, target, sem):
    core, y_low, z, x, y_half = places()
    block = pieces[0].shape[1]
    left, right = lax.rem(x + 3, 4), lax.rem(x + 1, 4)
    come, back = jnp.where(core == 0, left, right), jnp.where(core == 0, right, left)
    across = lax.rem(x + 2, 4)
    other = 1 - core
    spots = [
        (core, x), (other, x), (core, come), (other, come),
        (other, back), (core, back), (core, across), (other, across),
    ]
    copies = []
    for array, (slot, place) in zip(pieces, spots):
        for k in range(2):
            start = (lax.rem(y_low + k, 2) * 4 + place) * block
            spot = pl.ds(pl.multiple_of(start, block), block)
            copies.append(pltpu.make_async_copy(array.at[k], target.at[slot, spot, :], sem.at[len(copies)]))
    return copies


def side_copies(own, near, swapped, far, target, sem):
    core, y_low, z, x, y_half = places()
    block = own.shape[1]
    down, up = lax.rem(z + 3, 4), lax.rem(z + 1, 4)
    come, back = jnp.where(core == 0, down, up), jnp.where(core == 0, up, down)
    copies = []
    for array, place in ((own, z), (near, come), (swapped, back), (far, lax.rem(z + 2, 4))):
        for k in range(2):
            start = (place * 2 + lax.rem(y_half + k, 2)) * block
            spot = pl.ds(pl.multiple_of(start, block), block)
            copies.append(pltpu.make_async_copy(array.at[k], target.at[spot, :], sem.at[16 + len(copies)]))
    return copies


def main_kernel(
    rank_t, rank_i, rank_j, rank_s, low_inv_hbm, sketch_t_hbm, y_t_hbm, x_t_hbm, tile_u_hbm, tile_v_hbm,
    row0, row1, row2, row3, row4, row5, row6, row7, side_own, side_near, side_swapped, side_far,
    out_u_hbm, out_v_hbm,
    low_inv, sketch_t, y_t, x_t, tile_u, tile_v, panel, col_uv, up, wide_u, out_u, out_v, aug_ref, w_t, g_t, p_ref,
    in_sem, out_sem
):
    rows = tile_u.shape[0]
    t_rank, i_rank, j_rank, s_rank = rank_t[0, 0], rank_i[0], rank_j[0], rank_s[0, 0]
    first = side_copies(side_own, side_near, side_swapped, side_far, col_uv, in_sem)
    pairs = [
        (tile_v_hbm, tile_v), (low_inv_hbm, low_inv), (sketch_t_hbm, sketch_t),
        (tile_u_hbm, tile_u), (y_t_hbm, y_t), (x_t_hbm, x_t),
    ]
    kept = [pltpu.make_async_copy(source, target, in_sem.at[24 + k]) for k, (source, target) in enumerate(pairs)]
    first += kept[:3]
    then = panel_copies((row0, row1, row2, row3, row4, row5, row6, row7), panel, in_sem) + kept[3:]
    for load in first + then:
        load.start()
    for load in first:
        load.wait()
    sides = col_uv[...]
    keep = (iota((64, 256), 0) < j_rank) & (iota((64, 256), 1) < t_rank)
    side = jnp.where(keep, -tn(sides, tile_v[...])[:64], 0.0)
    corner, dead = masked_gram(tn(sides, sides)[:64, :64], j_rank)
    low_pt = nt(side, low_inv[...])
    schur = corner + dead - nt(low_pt, low_pt)
    for load in then:
        load.wait()
    keep_i = (iota((64, 256), 0) < j_rank) & (iota((64, 256), 1) < i_rank)
    cross_t = jnp.where(keep_i, tn(sides, panel[1])[64:], 0.0).astype(BF16)
    eye = (iota((64, 64), 0) == iota((64, 64), 1)).astype(F32)
    start = jnp.concatenate([eye, schur], axis=1)
    low_pp = lower_only(nt(start, shifted(leaf(start))))
    for step in range(rows // CHUNK):
        here = slice(step * CHUNK, step * CHUNK + CHUNK)
        top, rest = halves(nt(panel[0, here, :], cross_t, None))
        up[here, :] = jnp.concatenate([top, rest, top, rest], axis=1)
        part = col_uv[here, :][:, :64]
        wide_u[here, :] = jnp.concatenate([part, part], axis=1)
    both = tn(up[:, :128], tile_u[...])
    gram_pt = jnp.where(keep, both[:64] + both[64:], 0.0)
    four = tn(up[:, :128], up[:, :128])
    four = four[:64] + four[64:]
    gram_pp = (four + pltpu.roll(four, 64, 1))[:, :64]
    drawn = iota((256, 256), 0) < s_rank
    ys = jnp.where(drawn, y_t[...], 0.0)
    yp = nt(sketch_t[:, :256], low_pt) + nt(sketch_t[:, 256:], low_pp)
    yp = jnp.where((iota((256, 64), 1) < j_rank) & (iota((256, 64), 0) < s_rank), yp, 0.0)
    xs = jnp.where(drawn, x_t[...], 0.0) + nn(yp, gram_pt)
    xp = nt(ys, gram_pt) + nn(yp, gram_pp)
    same = iota((256, 256), 0) == iota((256, 256), 1)
    dead = (same & (iota((256, 256), 0) >= s_rank)).astype(F32)
    spread(nt(xs, ys) + nt(xp, yp) + dead, aug_ref)
    factor(aug_ref)
    inverse = gather_inverse(aug_ref)
    w_t[...] = nn(inverse, ys)
    g_t[...] = nn(inverse, xs)
    p_ref[...] = nn(inverse, jnp.concatenate([yp, xp], axis=1))
    live = (same & (iota((256, 256), 0) < s_rank)).astype(F32)

    def refine(state):
        count, unused = state
        pair = p_ref[...]
        upper = jnp.where(iota(pair.shape, 1) < 64, pair, 0.0)
        error = nt(w_t[...], g_t[...]) + nt(upper, pltpu.roll(pair, 64, 1)) - live
        size = jnp.max(jnp.sum(jnp.abs(error), axis=1, keepdims=True))
        step = (lower_only(error) - jnp.where(same, 0.5 * error, 0.0)).astype(BF16)
        for ref in (w_t, g_t, p_ref):
            ref[...] = ref[...] - nn(step, ref[...].astype(BF16), None)
        return count + 1, size

    lax.while_loop(lambda s: (s[0] < 12) & (s[1] > TOLERANCE), refine, (jnp.int32(0), jnp.float32(1.0)))
    scale = math.sqrt(rows)
    u_hi, u_lo = halves(w_t[...] * scale)
    pair = p_ref[...]
    p_hi, p_lo = halves(pair[:, :64] * scale)
    v_hi, v_lo = halves(g_t[...])
    u_all = jnp.concatenate([u_hi, u_lo, p_hi, p_hi, p_lo, p_lo], axis=1)
    v_all = jnp.concatenate([v_hi, v_lo, *halves(-pair[:, 64:])], axis=1)
    stores = []
    for step in range(rows // CHUNK):
        here = slice(step * CHUNK, step * CHUNK + CHUNK)
        tile = tile_u[here, :]
        out_u[here, :] = nt(jnp.concatenate([tile, tile, up[here, :]], axis=1), u_all, None)
        tile = tile_v[here, :]
        stores.append(pltpu.make_async_copy(out_u.at[here, :], out_u_hbm.at[here, :], out_sem.at[0, step]))
        stores[-1].start()
        out_v[here, :] = nt(jnp.concatenate([tile, tile, wide_u[here, :]], axis=1), v_all, None)
        stores.append(pltpu.make_async_copy(out_v.at[here, :], out_v_hbm.at[here, :], out_sem.at[1, step]))
        stores[-1].start()
    for store in stores:
        store.wait()


def main_call(ranks, low_inv, sketch_t, y_t, x_t, tile_u, tile_v, panels, sides):
    rows = tile_u.shape[0]
    hbm = pl.BlockSpec(memory_space=pl.ANY)
    out = jax.ShapeDtypeStruct((rows, 256), F32)
    block = pltpu.VMEM((256, 256), F32)
    wide = pltpu.VMEM((rows, 256), BF16)
    half = pltpu.VMEM((rows, 128), BF16)
    result = pltpu.VMEM((rows, 256), F32)
    return pl.pallas_call(
        main_kernel,
        out_shape=(out, out),
        in_specs=[pl.BlockSpec(memory_space=pltpu.SMEM)] * 4 + [hbm] * 18,
        out_specs=(hbm, hbm),
        scratch_shapes=[
            block, pltpu.VMEM((256, 320), F32), block, block, wide, wide, pltpu.VMEM((2, rows, 256), BF16), half, wide, half, result, result,
            pltpu.VMEM((256, 512), F32), block, block, pltpu.VMEM((256, 128), F32),
            pltpu.SemaphoreType.DMA((30,)), pltpu.SemaphoreType.DMA((2, rows // CHUNK)),
        ],
        compiler_params=pltpu.CompilerParams(vmem_limit_bytes=VMEM_LIMIT),
        cost_estimate=pl.CostEstimate(flops=20 * 10**9, bytes_accessed=15 * 10**6, transcendentals=0),
        name="recompress",
    )(*ranks, low_inv, sketch_t, y_t, x_t, tile_u, tile_v, *panels, *sides)


def send(x, axis, count, step):
    return lax.ppermute(x, axis, [(i, step(i)) for i in range(count)])


def swap(x):
    return send(x, "col", 16, lambda i: i ^ 1)


def round_x(x):
    return send(x, "col", 16, lambda i: i // 8 * 8 + (i + (2 if i % 2 == 0 else 6)) % 8)


def round_z(x):
    return send(x, ("row", "col"), 128, lambda i: (i + (32 if i % 2 == 0 else 96)) % 128)


def body(tile_u, tile_v, row_u, row_v, col_u, col_v, tile_rank, row_rank, col_rank, target_rank, sketch):
    first = lax.axis_index("col") % 2 == 0
    own_u, own_v = tile_u[0, 0], tile_v[0, 0]
    side = jnp.concatenate([col_u[0], col_v[0]], axis=1)
    give = jnp.where(first, row_v[0], row_u[0])
    keep = jnp.where(first, row_u[0], row_v[0])
    got = swap(give)
    chip = jnp.concatenate([jnp.where(first, keep, got), jnp.where(first, got, keep)], axis=0)
    chip, side = lax.optimization_barrier((chip, side))
    chip_other = send(chip, "col", 16, lambda i: i ^ 8)
    side_other = send(side, "row", 8, lambda i: i ^ 1)
    chip_swapped, side_swapped = swap(chip), swap(side)
    early = early_call(tile_rank, sketch, own_u, own_v)
    early, side_other, chip_other, chip_swapped, side_swapped = lax.optimization_barrier(
        (early, side_other, chip_other, chip_swapped, side_swapped)
    )
    gram, sketch_t, aug, low0 = early
    mine = jnp.stack([chip, chip_other])
    side_all = jnp.stack([side, side_other, side_swapped, swap(side_other)])
    near = round_x(mine)
    theirs = jnp.stack([chip_swapped, swap(chip_other)])
    near_theirs = round_x(theirs)
    side_near = round_z(side_all)
    aug, low1, low2 = middle_call(aug)
    aug, near, side_near = lax.optimization_barrier((aug, near, side_near))
    far, side_far = round_x(near), round_z(side_near[:2])
    near_swapped, side_back = swap(near), swap(side_near[2:])
    low_inv, y_t, x_t = late_call(tile_rank, aug, low0, low1, low2, sketch_t, gram)
    theirs_swapped = swap(near_theirs)
    far, side_far, near_swapped, side_back, theirs_swapped, y_t, row_rank, col_rank, target_rank = lax.optimization_barrier(
        (far, side_far, near_swapped, side_back, theirs_swapped, y_t, row_rank, col_rank, target_rank)
    )
    ranks = (tile_rank, row_rank, col_rank, target_rank)
    panels = [mine, theirs, near, near_theirs, near_swapped, theirs_swapped, far, swap(far)]
    sides = [side_all, side_near, side_back, side_far]
    new_u, new_v = main_call(ranks, low_inv, sketch_t, y_t, x_t, own_u, own_v, panels, sides)
    return (new_u[None, None], new_v[None, None])


def solution(mesh):
    placed = (
        P("row", "col", None, None),
        P("row", "col", None, None),
        P("row", "col", None),
        P("row", "col", None),
        P("col", "row", None),
        P("col", "row", None),
        P("row", "col"),
        P("row"),
        P("col"),
        P("row", "col"),
        P(),
    )
    return jax.shard_map(
        body,
        mesh=mesh,
        in_specs=placed,
        out_specs=(P("row", "col", None, None), P("row", "col", None, None)),
        check_vma=False,
    )
```

```python
import math

import jax
import jax.numpy as jnp
from jax import lax
from jax.experimental import pallas as pl
from jax.experimental.pallas import tpu as pltpu
from jax.sharding import PartitionSpec as P

F32 = jnp.float32
BF16 = jnp.bfloat16
HIGH = lax.Precision.HIGHEST
CHUNK = 672
TOLERANCE = 3e-4
VMEM_LIMIT = 60 * 1024 * 1024


def nn(a, b, precision=HIGH):
    return lax.dot_general(a, b, (((1,), (0,)), ((), ())), precision=precision, preferred_element_type=F32)


def nt(a, b, precision=HIGH):
    return lax.dot_general(a, b, (((1,), (1,)), ((), ())), precision=precision, preferred_element_type=F32)


def tn(a, b, precision=None):
    return lax.dot_general(a, b, (((0,), (0,)), ((), ())), precision=precision, preferred_element_type=F32)


def lane_splat(x, lane):
    return jnp.broadcast_to(x[:, lane : lane + 1], x.shape)


def row_splat(x, row):
    return jnp.broadcast_to(x[row : row + 1, :], x.shape)


def total(terms):
    while len(terms) > 1:
        terms = [terms[k] + terms[k + 1] if k + 1 < len(terms) else terms[k] for k in range(0, len(terms), 2)]
    return terms[0]


def leaf(block):
    count = 8
    rows = [block[8 * r : 8 * r + 8, :] for r in range(count)]
    sub = lax.broadcasted_iota(jnp.int32, (8, 128), 0)
    diag = [lane_splat(rows[0], 64 + m) for m in range(8)]
    for b in range(count):
        more = b + 1 < count
        x = rows[b]
        if more:
            ahead = rows[b + 1]
            side = [lane_splat(ahead, 64 + 8 * b + m) for m in range(8)]
            following = [lane_splat(ahead, 72 + 8 * b + m) for m in range(8)]
        far = {r: [lane_splat(rows[r], 64 + 8 * b + m) for m in range(8)] for r in range(b + 2, count)}
        inverse, pivot_rows, low = [], [], []
        pivots = diag[0]
        for k in range(8):
            r = 1.0 / row_splat(diag[k], k)
            inverse.append(r)
            if k:
                pivots = jnp.where(sub == k, diag[k], pivots)
            below = jnp.where(sub > k, diag[k], 0.0)
            low.append(below)
            pivot = row_splat(x, k) * r
            pivot_rows.append(pivot)
            for m in range(k + 1, 8):
                entry = row_splat(diag[m], k)
                diag[m] = diag[m] - (below * entry) * r
                if more:
                    side[m] = side[m] - side[k] * (entry * r)
            x = x - below * pivot
            if more:
                ahead = ahead - side[k] * pivot
        if more:
            scaled = [side[k] * inverse[k] for k in range(8)]
            diag = [
                following[m] - total([scaled[k] * row_splat(side[k], m) for k in range(8)]) for m in range(8)
            ]
            rows[b + 1] = ahead
        if far:
            back = [None] * 8
            for k in range(7, -1, -1):
                column = low[k] * inverse[k]
                back[k] = pivot_rows[k]
                for i in range(k + 1, 8):
                    back[k] = back[k] - row_splat(column, i) * back[i]
            for r in far:
                rows[r] = rows[r] - total([far[r][m] * back[m] for m in range(8)])
        rows[b] = x * lax.rsqrt(pivots)
    return jnp.concatenate(rows, axis=0)


def shifted(pair):
    lane = lax.broadcasted_iota(jnp.int32, pair.shape, 1)
    return jnp.where(lane >= 64, pltpu.roll(pair, 64, 1), 0.0)


def spread(matrix, aug_ref):
    size = matrix.shape[0]
    lane = lax.broadcasted_iota(jnp.int32, (size, 128), 1)
    row = lax.broadcasted_iota(jnp.int32, (size, 128), 0)
    for k in range(size // 64):
        half = matrix[:, 128 * (k // 2) : 128 * (k // 2) + 128]
        if k % 2 == 0:
            half = pltpu.roll(half, 64, 1)
        eye = (row == lane + 64 * k).astype(F32)
        aug_ref[:, 128 * k : 128 * k + 128] = jnp.where(lane >= 64, half, eye)


def gather_inverse(aug_ref):
    lane = lax.broadcasted_iota(jnp.int32, (aug_ref.shape[0], 128), 1)
    parts = []
    for t in range(aug_ref.shape[1] // 256):
        even = aug_ref[:, 256 * t : 256 * t + 128]
        odd = aug_ref[:, 256 * t + 128 : 256 * t + 256]
        parts.append(jnp.where(lane < 64, even, pltpu.roll(odd, 64, 1)))
    return jnp.concatenate(parts, axis=1)


def factor(aug_ref, low_refs=None, begin=0, end=None, start=None):
    size = aug_ref.shape[0]
    count = size // 64
    if start is None:
        start = aug_ref[:64, :128]
    for k in range(begin, count if end is None else end):
        here = slice(64 * k, 64 * k + 64)
        tile = slice(128 * k, 128 * k + 128)
        pair = leaf(start)
        wide = shifted(pair)
        inverse = pair[:, :64]
        if low_refs is not None:
            low_refs[k][here, :] = nt(start, wide)
        if k + 1 == count:
            aug_ref[here, :] = nn(inverse, aug_ref[here, :])
            break
        below = slice(64 * k + 64, 64 * k + 128)
        after = slice(128 * k + 128, 128 * k + 256)
        near = nt(aug_ref[below, tile], wide)
        start = aug_ref[below, after] - nn(near, nn(inverse, aug_ref[here, after]))
        ahead = nn(inverse, aug_ref[here, :])
        left = nt(aug_ref[64 * k + 64 :, tile], wide)
        aug_ref[here, :] = ahead
        if low_refs is not None:
            low_refs[k][64 * k + 64 :, :] = left
        aug_ref[64 * k + 64 :, :] = aug_ref[64 * k + 64 :, :] - nn(left, ahead)
    return start


def masked_gram(gram, rank):
    size = gram.shape[0]
    row = lax.broadcasted_iota(jnp.int32, gram.shape, 0)
    col = lax.broadcasted_iota(jnp.int32, gram.shape, 1)
    both = (row < rank) & (col < rank)
    dead = (row == col) & (row >= rank)
    return jnp.where(both, gram, 0.0), dead.astype(F32)


def iota(shape, dim):
    return lax.broadcasted_iota(jnp.int32, shape, dim)


def halves(x):
    top = x.astype(BF16)
    return top, (x - top.astype(F32)).astype(BF16)


def lower_only(x):
    return jnp.where(iota(x.shape, 0) >= iota(x.shape, 1), x, 0.0)


def places():
    spot_i, spot_j = lax.axis_index("row"), lax.axis_index("col")
    return lax.rem(spot_j, 2), spot_j // 8, spot_i // 2, lax.rem(spot_j // 2, 4), lax.rem(spot_i, 2)


def copy_all(pairs, sem):
    copies = [pltpu.make_async_copy(source, target, sem.at[k]) for k, (source, target) in enumerate(pairs)]
    for copy in copies:
        copy.start()
    return copies


def early_kernel(
    rank_t, sketch_hbm, tile_u_hbm, tile_v_hbm,
    gram_hbm, sketch_t_hbm, aug_hbm, low0_hbm,
    sketch, tile_u, tile_v, gram, sketch_t, aug_ref, low0, in_sem, out_sem
):
    loads = copy_all([(tile_v_hbm, tile_v), (tile_u_hbm, tile_u), (sketch_hbm, sketch)], in_sem)
    rank = rank_t[0, 0]
    loads[0].wait()
    gram_v, dead = masked_gram(tn(tile_v[...], tile_v[...]), rank)
    spread(gram_v + dead, aug_ref)
    loads[1].wait()
    loads[2].wait()
    flipped = sketch[...].T
    sketch_t[...] = flipped
    gram[...] = masked_gram(tn(tile_u[...], tile_u[...]), rank)[0]
    stores = [
        pltpu.make_async_copy(source, target, out_sem.at[k])
        for k, (source, target) in enumerate([(gram, gram_hbm), (sketch_t, sketch_t_hbm), (low0, low0_hbm), (aug_ref, aug_hbm)])
    ]
    stores[0].start()
    stores[1].start()
    factor(aug_ref, (low0,), 0, 1)
    stores[2].start()
    stores[3].start()
    for store in stores:
        store.wait()


def early_call(rank, sketch, tile_u, tile_v):
    wide = pltpu.VMEM(tile_u.shape, BF16)
    hbm = pl.BlockSpec(memory_space=pl.ANY)
    shapes = [(256, 256), (256, 320), (256, 512), (256, 64)]
    return pl.pallas_call(
        early_kernel,
        out_shape=[jax.ShapeDtypeStruct(shape, F32) for shape in shapes],
        in_specs=[pl.BlockSpec(memory_space=pltpu.SMEM)] + [hbm] * 3,
        out_specs=[hbm] * 4,
        scratch_shapes=[pltpu.VMEM((320, 256), F32), wide, wide]
        + [pltpu.VMEM(shape, F32) for shape in shapes]
        + [pltpu.SemaphoreType.DMA((3,)), pltpu.SemaphoreType.DMA((4,))],
        compiler_params=pltpu.CompilerParams(vmem_limit_bytes=VMEM_LIMIT),
        cost_estimate=pl.CostEstimate(flops=7 * 10**9, bytes_accessed=4 * 10**6, transcendentals=0),
        name="early_factor",
    )(rank, sketch, tile_u, tile_v)


def middle_kernel(aug_hbm, aug_out_hbm, low1_hbm, low2_hbm, aug_ref, low1, low2, in_sem, out_sem):
    load = pltpu.make_async_copy(aug_hbm, aug_ref, in_sem)
    load.start()
    low1[:64, :] = jnp.zeros((64, 64), F32)
    low2[:128, :] = jnp.zeros((128, 64), F32)
    load.wait()
    factor(aug_ref, (None, low1, low2), 1, 3, aug_ref[64:128, 128:256])
    for store in copy_all([(aug_ref, aug_out_hbm), (low1, low1_hbm), (low2, low2_hbm)], out_sem):
        store.wait()


def middle_call(aug):
    hbm = pl.BlockSpec(memory_space=pl.ANY)
    shapes = [(256, 512), (256, 64), (256, 64)]
    return pl.pallas_call(
        middle_kernel,
        out_shape=[jax.ShapeDtypeStruct(shape, F32) for shape in shapes],
        in_specs=[hbm],
        out_specs=[hbm] * 3,
        scratch_shapes=[pltpu.VMEM(shape, F32) for shape in shapes] + [pltpu.SemaphoreType.DMA, pltpu.SemaphoreType.DMA((3,))],
        compiler_params=pltpu.CompilerParams(vmem_limit_bytes=VMEM_LIMIT),
        cost_estimate=pl.CostEstimate(flops=6 * 10**9, bytes_accessed=2 * 10**6, transcendentals=0),
        name="middle_factor",
    )(aug)


def late_kernel(
    rank_t, aug_hbm, low0_hbm, low1_hbm, low2_hbm, sketch_t_hbm, gram_hbm,
    low_inv_hbm, y_hbm, x_hbm,
    aug_ref, low0, low1, low2, sketch_t, gram, low3, low_inv, y_ref, x_ref, in_sem, out_sem,
):
    pairs = [(aug_hbm, aug_ref), (low0_hbm, low0), (low1_hbm, low1), (low2_hbm, low2), (sketch_t_hbm, sketch_t), (gram_hbm, gram)]
    loads = copy_all(pairs, in_sem)
    low3[:192, :] = jnp.zeros((192, 64), F32)
    loads[0].wait()
    lows = (low0, low1, low2, low3)
    factor(aug_ref, lows, 3, 4, aug_ref[192:256, 384:512])
    low_inv[...] = gather_inverse(aug_ref)
    first = pltpu.make_async_copy(low_inv, low_inv_hbm, out_sem.at[2])
    first.start()
    for load in loads[1:]:
        load.wait()
    low = lower_only(jnp.concatenate([ref[...] for ref in lows], axis=1))
    y = jnp.where(iota((256, 256), 1) < rank_t[0, 0], nt(sketch_t[:, :256], low), 0.0)
    y_ref[...] = y
    x_ref[...] = nn(y, gram[...])
    for store in copy_all([(y_ref, y_hbm), (x_ref, x_hbm)], out_sem) + [first]:
        store.wait()


def late_call(rank, aug, low0, low1, low2, sketch_t, gram):
    hbm = pl.BlockSpec(memory_space=pl.ANY)
    square = jax.ShapeDtypeStruct((256, 256), F32)
    block, thin = pltpu.VMEM((256, 256), F32), pltpu.VMEM((256, 64), F32)
    return pl.pallas_call(
        late_kernel,
        out_shape=[square] * 3,
        in_specs=[pl.BlockSpec(memory_space=pltpu.SMEM)] + [hbm] * 6,
        out_specs=[hbm] * 3,
        scratch_shapes=[pltpu.VMEM((256, 512), F32), thin, thin, thin, pltpu.VMEM((256, 320), F32), block, thin, block, block, block]
        + [pltpu.SemaphoreType.DMA((6,)), pltpu.SemaphoreType.DMA((3,))],
        compiler_params=pltpu.CompilerParams(vmem_limit_bytes=VMEM_LIMIT),
        cost_estimate=pl.CostEstimate(flops=6 * 10**9, bytes_accessed=2 * 10**6, transcendentals=0),
        name="late_factor",
    )(rank, aug, low0, low1, low2, sketch_t, gram)


def panel_copies(pieces, target, sem):
    core, y_low, z, x, y_half = places()
    block = pieces[0].shape[1]
    left, right = lax.rem(x + 3, 4), lax.rem(x + 1, 4)
    come, back = jnp.where(core == 0, left, right), jnp.where(core == 0, right, left)
    across = lax.rem(x + 2, 4)
    other = 1 - core
    spots = [
        (core, x), (other, x), (core, come), (other, come),
        (other, back), (core, back), (core, across), (other, across),
    ]
    copies = []
    for array, (slot, place) in zip(pieces, spots):
        for k in range(2):
            start = (lax.rem(y_low + k, 2) * 4 + place) * block
            spot = pl.ds(pl.multiple_of(start, block), block)
            copies.append(pltpu.make_async_copy(array.at[k], target.at[slot, spot, :], sem.at[len(copies)]))
    return copies


def side_copies(own, near, swapped, far, target, sem):
    core, y_low, z, x, y_half = places()
    block = own.shape[1]
    down, up = lax.rem(z + 3, 4), lax.rem(z + 1, 4)
    come, back = jnp.where(core == 0, down, up), jnp.where(core == 0, up, down)
    copies = []
    for array, place in ((own, z), (near, come), (swapped, back), (far, lax.rem(z + 2, 4))):
        for k in range(2):
            start = (place * 2 + lax.rem(y_half + k, 2)) * block
            spot = pl.ds(pl.multiple_of(start, block), block)
            copies.append(pltpu.make_async_copy(array.at[k], target.at[spot, :], sem.at[16 + len(copies)]))
    return copies


def main_kernel(
    rank_t, rank_i, rank_j, rank_s, low_inv_hbm, sketch_t_hbm, y_t_hbm, x_t_hbm, tile_u_hbm, tile_v_hbm,
    row0, row1, row2, row3, row4, row5, row6, row7, side_own, side_near, side_swapped, side_far,
    out_u_hbm, out_v_hbm,
    low_inv, sketch_t, y_t, x_t, tile_u, tile_v, panel, col_uv, up, wide_u, out_u, out_v, aug_ref, w_t, g_t, p_ref,
    in_sem, out_sem
):
    rows = tile_u.shape[0]
    t_rank, i_rank, j_rank, s_rank = rank_t[0, 0], rank_i[0], rank_j[0], rank_s[0, 0]
    first = side_copies(side_own, side_near, side_swapped, side_far, col_uv, in_sem)
    pairs = [
        (tile_v_hbm, tile_v), (low_inv_hbm, low_inv), (sketch_t_hbm, sketch_t),
        (tile_u_hbm, tile_u), (y_t_hbm, y_t), (x_t_hbm, x_t),
    ]
    kept = [pltpu.make_async_copy(source, target, in_sem.at[24 + k]) for k, (source, target) in enumerate(pairs)]
    first += kept[:3]
    then = panel_copies((row0, row1, row2, row3, row4, row5, row6, row7), panel, in_sem) + kept[3:]
    for load in first + then:
        load.start()
    for load in first:
        load.wait()
    sides = col_uv[...]
    keep = (iota((64, 256), 0) < j_rank) & (iota((64, 256), 1) < t_rank)
    side = jnp.where(keep, -tn(sides, tile_v[...])[:64], 0.0)
    corner, dead = masked_gram(tn(sides, sides)[:64, :64], j_rank)
    low_pt = nt(side, low_inv[...])
    schur = corner + dead - nt(low_pt, low_pt)
    for load in then:
        load.wait()
    keep_i = (iota((64, 256), 0) < j_rank) & (iota((64, 256), 1) < i_rank)
    cross_t = jnp.where(keep_i, tn(sides, panel[1])[64:], 0.0).astype(BF16)
    eye = (iota((64, 64), 0) == iota((64, 64), 1)).astype(F32)
    start = jnp.concatenate([eye, schur], axis=1)
    low_pp = lower_only(nt(start, shifted(leaf(start))))
    for step in range(rows // CHUNK):
        here = slice(step * CHUNK, step * CHUNK + CHUNK)
        top, rest = halves(nt(panel[0, here, :], cross_t, None))
        up[here, :] = jnp.concatenate([top, rest, top, rest], axis=1)
        part = col_uv[here, :][:, :64]
        wide_u[here, :] = jnp.concatenate([part, part], axis=1)
    both = tn(up[:, :128], tile_u[...])
    gram_pt = jnp.where(keep, both[:64] + both[64:], 0.0)
    four = tn(up[:, :128], up[:, :128])
    four = four[:64] + four[64:]
    gram_pp = (four + pltpu.roll(four, 64, 1))[:, :64]
    drawn = iota((256, 256), 0) < s_rank
    ys = jnp.where(drawn, y_t[...], 0.0)
    yp = nt(sketch_t[:, :256], low_pt) + nt(sketch_t[:, 256:], low_pp)
    yp = jnp.where((iota((256, 64), 1) < j_rank) & (iota((256, 64), 0) < s_rank), yp, 0.0)
    xs = jnp.where(drawn, x_t[...], 0.0) + nn(yp, gram_pt)
    xp = nt(ys, gram_pt) + nn(yp, gram_pp)
    same = iota((256, 256), 0) == iota((256, 256), 1)
    dead = (same & (iota((256, 256), 0) >= s_rank)).astype(F32)
    spread(nt(xs, ys) + nt(xp, yp) + dead, aug_ref)
    factor(aug_ref)
    inverse = gather_inverse(aug_ref)
    w_t[...] = nn(inverse, ys)
    g_t[...] = nn(inverse, xs)
    p_ref[...] = nn(inverse, jnp.concatenate([yp, xp], axis=1))
    live = (same & (iota((256, 256), 0) < s_rank)).astype(F32)

    def refine(state):
        count, unused = state
        pair = p_ref[...]
        upper = jnp.where(iota(pair.shape, 1) < 64, pair, 0.0)
        error = nt(w_t[...], g_t[...]) + nt(upper, pltpu.roll(pair, 64, 1)) - live
        size = jnp.max(jnp.sum(jnp.abs(error), axis=1, keepdims=True))
        step = (lower_only(error) - jnp.where(same, 0.5 * error, 0.0)).astype(BF16)
        for ref in (w_t, g_t, p_ref):
            ref[...] = ref[...] - nn(step, ref[...].astype(BF16), None)
        return count + 1, size

    lax.while_loop(lambda s: (s[0] < 12) & (s[1] > TOLERANCE), refine, (jnp.int32(0), jnp.float32(1.0)))
    scale = math.sqrt(rows)
    u_hi, u_lo = halves(w_t[...] * scale)
    pair = p_ref[...]
    p_hi, p_lo = halves(pair[:, :64] * scale)
    v_hi, v_lo = halves(g_t[...])
    u_all = jnp.concatenate([u_hi, u_lo, p_hi, p_hi, p_lo, p_lo], axis=1)
    v_all = jnp.concatenate([v_hi, v_lo, *halves(-pair[:, 64:])], axis=1)
    stores = []
    for step in range(rows // CHUNK):
        here = slice(step * CHUNK, step * CHUNK + CHUNK)
        tile = tile_u[here, :]
        out_u[here, :] = nt(jnp.concatenate([tile, tile, up[here, :]], axis=1), u_all, None)
        tile = tile_v[here, :]
        stores.append(pltpu.make_async_copy(out_u.at[here, :], out_u_hbm.at[here, :], out_sem.at[0, step]))
        stores[-1].start()
        out_v[here, :] = nt(jnp.concatenate([tile, tile, wide_u[here, :]], axis=1), v_all, None)
        stores.append(pltpu.make_async_copy(out_v.at[here, :], out_v_hbm.at[here, :], out_sem.at[1, step]))
        stores[-1].start()
    for store in stores:
        store.wait()


def main_call(ranks, low_inv, sketch_t, y_t, x_t, tile_u, tile_v, panels, sides):
    rows = tile_u.shape[0]
    hbm = pl.BlockSpec(memory_space=pl.ANY)
    out = jax.ShapeDtypeStruct((rows, 256), F32)
    block = pltpu.VMEM((256, 256), F32)
    wide = pltpu.VMEM((rows, 256), BF16)
    half = pltpu.VMEM((rows, 128), BF16)
    result = pltpu.VMEM((rows, 256), F32)
    return pl.pallas_call(
        main_kernel,
        out_shape=(out, out),
        in_specs=[pl.BlockSpec(memory_space=pltpu.SMEM)] * 4 + [hbm] * 18,
        out_specs=(hbm, hbm),
        scratch_shapes=[
            block, pltpu.VMEM((256, 320), F32), block, block, wide, wide, pltpu.VMEM((2, rows, 256), BF16), half, wide, half, result, result,
            pltpu.VMEM((256, 512), F32), block, block, pltpu.VMEM((256, 128), F32),
            pltpu.SemaphoreType.DMA((30,)), pltpu.SemaphoreType.DMA((2, rows // CHUNK)),
        ],
        compiler_params=pltpu.CompilerParams(vmem_limit_bytes=VMEM_LIMIT),
        cost_estimate=pl.CostEstimate(flops=20 * 10**9, bytes_accessed=15 * 10**6, transcendentals=0),
        name="recompress",
    )(*ranks, low_inv, sketch_t, y_t, x_t, tile_u, tile_v, *panels, *sides)


def send(x, axis, count, step):
    return lax.ppermute(x, axis, [(i, step(i)) for i in range(count)])


def swap(x):
    return send(x, "col", 16, lambda i: i ^ 1)


def round_x(x):
    return send(x, "col", 16, lambda i: i // 8 * 8 + (i + (2 if i % 2 == 0 else 6)) % 8)


def round_z(x):
    return send(x, ("row", "col"), 128, lambda i: (i + (32 if i % 2 == 0 else 96)) % 128)


def body(tile_u, tile_v, row_u, row_v, col_u, col_v, tile_rank, row_rank, col_rank, target_rank, sketch):
    first = lax.axis_index("col") % 2 == 0
    own_u, own_v = tile_u[0, 0], tile_v[0, 0]
    side = jnp.concatenate([col_u[0], col_v[0]], axis=1)
    give = jnp.where(first, row_v[0], row_u[0])
    keep = jnp.where(first, row_u[0], row_v[0])
    got = swap(give)
    chip = jnp.concatenate([jnp.where(first, keep, got), jnp.where(first, got, keep)], axis=0)
    chip, side = lax.optimization_barrier((chip, side))
    chip_other = send(chip, "col", 16, lambda i: i ^ 8)
    side_other = send(side, "row", 8, lambda i: i ^ 1)
    chip_swapped, side_swapped = swap(chip), swap(side)
    early = early_call(tile_rank, sketch, own_u, own_v)
    early, side_other, chip_other, chip_swapped, side_swapped = lax.optimization_barrier(
        (early, side_other, chip_other, chip_swapped, side_swapped)
    )
    gram, sketch_t, aug, low0 = early
    mine = jnp.stack([chip, chip_other])
    side_all = jnp.stack([side, side_other, side_swapped, swap(side_other)])
    near = round_x(mine)
    theirs = jnp.stack([chip_swapped, swap(chip_other)])
    near_theirs = round_x(theirs)
    side_near = round_z(side_all)
    aug, low1, low2 = middle_call(aug)
    aug, near, side_near = lax.optimization_barrier((aug, near, side_near))
    far, side_far = round_x(near), round_z(side_near[:2])
    near_swapped, side_back = swap(near), swap(side_near[2:])
    low_inv, y_t, x_t = late_call(tile_rank, aug, low0, low1, low2, sketch_t, gram)
    theirs_swapped = swap(near_theirs)
    far, side_far, near_swapped, side_back, theirs_swapped, y_t, row_rank, col_rank, target_rank = lax.optimization_barrier(
        (far, side_far, near_swapped, side_back, theirs_swapped, y_t, row_rank, col_rank, target_rank)
    )
    ranks = (tile_rank, row_rank, col_rank, target_rank)
    panels = [mine, theirs, near, near_theirs, near_swapped, theirs_swapped, far, swap(far)]
    sides = [side_all, side_near, side_back, side_far]
    new_u, new_v = main_call(ranks, low_inv, sketch_t, y_t, x_t, own_u, own_v, panels, sides)
    return (new_u[None, None], new_v[None, None])


def solution(mesh):
    placed = (
        P("row", "col", None, None),
        P("row", "col", None, None),
        P("row", "col", None),
        P("row", "col", None),
        P("col", "row", None),
        P("col", "row", None),
        P("row", "col"),
        P("row"),
        P("col"),
        P("row", "col"),
        P(),
    )
    return jax.shard_map(
        body,
        mesh=mesh,
        in_specs=placed,
        out_specs=(P("row", "col", None, None), P("row", "col", None, None)),
        check_vma=False,
    )
```
